512 devices in a mesh: ctx: 16 (over z), chan: 32 (over y, x, core).
Axes of the slice: x: 4, y: 4, z: 16, core: 2. Of those that a mesh axis runs over, the one named last changes fastest.
Arguments:
- conv_input: bfloat16 [2048, 16384], P('ctx', 'chan'), may hold values from -6 to 6
- gate_input: bfloat16 [2048, 16384], P('ctx', 'chan'), may hold values from -6 to 6
- out_grad: bfloat16 [2048, 16384], P('ctx', 'chan'), may hold values from -6 to 6
- conv_weight: float32 [4, 16384], P(None, 'chan'), may hold values from -3 to 3
- conv_bias: float32 [16384], P('chan'), may hold values from -3 to 3
- proj_weight: bfloat16 [544, 16384], P(None, 'chan'), may hold values from -0.046875 to 0.046875
- step_weight: bfloat16 [512, 16384], P(None, 'chan'), may hold values from -0.25 to 0.25
- step_bias: float32 [16384], P('chan'), may hold values from -12 to -3
- decay_log: float32 [16, 16384], P(None, 'chan'), may hold values from -0.7 to 1.4
- skip_gain: float32 [16384], P('chan'), may hold values from 0.1 to 1.9
Outputs:
- grad_input: bfloat16 [2048, 16384], P('ctx', 'chan')
- grad_gate: bfloat16 [2048, 16384], P('ctx', 'chan')
- grad_proj: float32 [512, 16384], P('ctx', 'chan')
- grad_coef: float32 [32, 16384], P('ctx', 'chan')
- grad_step: float32 [512, 16384], P('ctx', 'chan')
- grad_conv_weight: float32 [4, 16384], P(None, 'chan')
- grad_conv_bias: float32 [16384], P('chan')
- grad_step_bias: float32 [16384], P('chan')
- grad_decay_log: float32 [16, 16384], P(None, 'chan')
- grad_skip: float32 [16384], P('chan')
The draws below stay inside these ranges and needn't reach their ends.
All inputs are finite; a program needn't handle non-finite values.
Results may differ from the reference program's by a relative error of at most 0.023.
Values may be sent and summed in bfloat16 or wider, within the bound.
A program may use at most 64 MiB of HBM per device.

```python
import jax
import jax.numpy as jnp
from jax import lax

DI = 16384
R = 512
N = 16
K = 4
PROJ = 544
TOKENS = 2048
N_CHAN = 32


def block_scale(stream_key, dims, split, least, largest):
    loudness = 1.0
    for dim, shards_of in split:
        heights = jax.random.uniform(jax.random.fold_in(jax.random.fold_in(stream_key, 6), dim), (shards_of,), jnp.float32, least / len(split), largest / len(split))
        loudness = loudness * jnp.repeat(jnp.exp(heights), dims[dim] // shards_of).reshape((-1,) + (1,) * (len(dims) - 1 - dim))
    return loudness


def centred(own_key, shape, deviation, most, split=(), dtype=jnp.bfloat16):
    factor_of = block_scale(own_key, shape, split, -0.22, 0.18) if split else 1.0
    drawn = jax.random.normal(own_key, shape, jnp.float32) * deviation * factor_of
    return jnp.minimum(jnp.maximum(drawn, -most), most).astype(dtype)


def setup_inputs(seed: int = 0) -> dict:
    splits = jax.random.split(jax.random.key(seed), 11)
    return {
        "conv_input": centred(splits[0], (TOKENS, DI), 1.0, 6.0, ((0, 16), (1, 32))),
        "gate_input": centred(splits[1], (TOKENS, DI), 1.0, 6.0, ((0, 16), (1, 32))),
        "out_grad": centred(splits[2], (TOKENS, DI), 1.0, 6.0, ((0, 16), (1, 32))),
        "conv_weight": centred(splits[3], (K, DI), K ** -0.5, 3.0, ((1, 32),), jnp.float32),
        "conv_bias": centred(splits[4], (DI,), 0.5, 3.0, ((0, 32),), jnp.float32),
        "proj_weight": centred(splits[5], (PROJ, DI), DI ** -0.5, 0.046875, ((1, 32),)),
        "step_weight": centred(splits[6], (R, DI), R ** -0.5, 0.25, ((1, 32),)),
        "step_bias": jnp.clip(-12.0 + 9.0 * jax.random.uniform(splits[7], (DI,), jnp.float32) ** block_scale(splits[7], (DI,), ((0, 32),), -0.2, 0.2), -12.0, -3.0),
        "decay_log": jnp.clip(-0.7 + 2.1 * jax.random.uniform(splits[8], (N, DI), jnp.float32) ** block_scale(splits[8], (N, DI), ((1, 32),), -0.2, 0.2), -0.7, 1.4),
        "skip_gain": jnp.clip(1.0 + 0.18 * jax.random.normal(splits[9], (DI,), jnp.float32), 0.1, 1.9),
    }


def silu_slope(values):
    sigma = jax.nn.sigmoid(values)
    return sigma * (1.0 + values * (1.0 - sigma))


def split_columns(array, pieces):
    piece_width = array.shape[-1] // pieces
    reshaped = array.reshape(array.shape[:-1] + (pieces, piece_width))
    return jnp.moveaxis(reshaped, -2, 0)


def join_columns(stacked):
    moved = jnp.moveaxis(stacked, 0, -2)
    return moved.reshape(moved.shape[:-2] + (moved.shape[-2] * moved.shape[-1],))


def conv_preact(inputs, weight, bias):
    length = inputs.shape[0]
    padded = jnp.pad(inputs.astype(jnp.float32), ((K - 1, 0), (0, 0)))
    result = jnp.zeros(inputs.shape, jnp.float32) + bias[None, :]
    for tap in range(K):
        result = result + weight[tap][None, :] * padded[tap:tap + length]
    return result


def reference(conv_input, gate_input, out_grad, conv_weight, conv_bias, proj_weight, step_weight, step_bias, decay_log, skip_gain):
    pieces = N_CHAN
    in_cols = split_columns(conv_input, pieces)
    gate_cols = split_columns(gate_input, pieces)
    grad_cols = split_columns(out_grad, pieces)
    conv_w_cols = split_columns(conv_weight, pieces)
    conv_b_cols = split_columns(conv_bias, pieces)
    proj_cols = split_columns(proj_weight, pieces)
    step_cols = split_columns(step_weight, pieces)
    bias_cols = split_columns(step_bias, pieces)
    decay_cols = split_columns(decay_log, pieces)
    skip_cols = split_columns(skip_gain, pieces)

    def project_piece(total, packed):
        in_part, w_part, b_part, p_part = packed
        conv_out = jax.nn.silu(conv_preact(in_part, w_part, b_part)).astype(jnp.bfloat16)
        term = lax.dot_general(conv_out, p_part, (((1,), (1,)), ((), ())), preferred_element_type=jnp.float32)
        return total + term, None

    projected_sum, _ = lax.scan(project_piece, jnp.zeros((TOKENS, PROJ), jnp.float32), (in_cols, conv_w_cols, conv_b_cols, proj_cols))
    projected = projected_sum.astype(jnp.bfloat16)
    step_low = projected[:, :R]
    input_coef = projected[:, R:R + N].astype(jnp.float32)
    output_coef = projected[:, R + N:].astype(jnp.float32)

    def scan_piece(total, packed):
        in_part, gate_part, grad_part, w_part, b_part, s_part, bias_part, decay_part, skip_part = packed
        conv_out = jax.nn.silu(conv_preact(in_part, w_part, b_part)).astype(jnp.bfloat16)
        conv_val = lax.optimization_barrier(conv_out).astype(jnp.float32)
        step_pre = jnp.dot(step_low, s_part, preferred_element_type=jnp.float32) + bias_part[None, :]
        step_size = jax.nn.softplus(step_pre)
        decay_rate = -jnp.exp(decay_part)
        scan_grad = grad_part.astype(jnp.float32) * jax.nn.silu(gate_part.astype(jnp.float32))
        zero_state = jnp.zeros((N, decay_part.shape[1]), jnp.float32)

        def forward_step(state, entry):
            size_now, conv_now, coef_now = entry
            state = jnp.exp(size_now[None, :] * decay_rate) * state + (size_now * conv_now)[None, :] * coef_now[:, None]
            return state, state

        _, history = lax.scan(forward_step, zero_state, (step_size, conv_val, input_coef))

        def adjoint_step(carried, entry):
            size_now, coef_now, grad_now = entry
            adjoint_now = coef_now[:, None] * grad_now[None, :] + carried
            return jnp.exp(size_now[None, :] * decay_rate) * adjoint_now, adjoint_now

        _, adjoint = lax.scan(adjoint_step, zero_state, (step_size, output_coef, scan_grad), reverse=True)
        prior = jnp.concatenate([zero_state[None], history[:-1]], axis=0)
        decayed = jnp.exp(step_size[:, None, :] * decay_rate[None]) * prior
        scan_out = jnp.sum(output_coef[:, :, None] * history, axis=1) + skip_part[None, :] * conv_val
        d_delta = jnp.sum(adjoint * (decay_rate[None] * decayed + input_coef[:, :, None] * conv_val[:, None, :]), axis=1)
        decay_grad = jnp.sum(adjoint * decayed * step_size[:, None, :], axis=0) * decay_rate
        coef_in_grad = jnp.sum(adjoint * (step_size * conv_val)[:, None, :], axis=2)
        coef_out_grad = jnp.sum(history * scan_grad[:, None, :], axis=2)
        conv_grad_scan = jnp.sum(adjoint * input_coef[:, :, None], axis=1) * step_size + skip_part[None, :] * scan_grad
        skip_grad = jnp.sum(scan_grad * conv_val, axis=0)
        gate_grad = (grad_part.astype(jnp.float32) * scan_out * silu_slope(gate_part.astype(jnp.float32))).astype(jnp.bfloat16)
        d_pre = d_delta * jax.nn.sigmoid(step_pre)
        bias_grad = jnp.sum(d_pre, axis=0)
        pre_bf = d_pre.astype(jnp.bfloat16)
        d_low = lax.dot_general(pre_bf, s_part, (((1,), (1,)), ((), ())), preferred_element_type=jnp.float32)
        step_grad = lax.dot_general(step_low, pre_bf, (((0,), (0,)), ((), ())), preferred_element_type=jnp.float32)
        total = total + jnp.concatenate([d_low, coef_in_grad, coef_out_grad], axis=1)
        return total, (gate_grad, conv_grad_scan, step_grad, decay_grad, bias_grad, skip_grad)

    back_sum, stacks = lax.scan(scan_piece, jnp.zeros((TOKENS, PROJ), jnp.float32), (in_cols, gate_cols, grad_cols, conv_w_cols, conv_b_cols, step_cols, bias_cols, decay_cols, skip_cols))
    gate_stack, scan_stack, step_stack, decay_stack, bias_stack, skip_stack = stacks
    back_proj = back_sum.astype(jnp.bfloat16)

    def conv_piece(packed):
        in_part, w_part, b_part, p_part, scan_part = packed
        conv_pre = conv_preact(in_part, w_part, b_part)
        conv_out = jax.nn.silu(conv_pre).astype(jnp.bfloat16)
        d_xc = scan_part + jnp.dot(back_proj, p_part, preferred_element_type=jnp.float32)
        proj_grad = lax.dot_general(back_proj, conv_out, (((0,), (0,)), ((), ())), preferred_element_type=jnp.float32)
        d_conv = d_xc * silu_slope(conv_pre)
        length = d_conv.shape[0]
        padded_in = jnp.pad(in_part.astype(jnp.float32), ((K - 1, 0), (0, 0)))
        padded_grad = jnp.pad(d_conv, ((0, K - 1), (0, 0)))
        conv_w_grad = jnp.stack([jnp.sum(d_conv * padded_in[tap:tap + length], axis=0) for tap in range(K)])
        input_grad = jnp.zeros(d_conv.shape, jnp.float32)
        for tap in range(K):
            input_grad = input_grad + w_part[tap][None, :] * padded_grad[K - 1 - tap:K - 1 - tap + length]
        return input_grad.astype(jnp.bfloat16), proj_grad, conv_w_grad, jnp.sum(d_conv, axis=0)

    input_stack, proj_stack, conv_w_stack, conv_b_stack = lax.map(conv_piece, (in_cols, conv_w_cols, conv_b_cols, proj_cols, scan_stack))
    return (join_columns(input_stack), join_columns(gate_stack), join_columns(proj_stack[:, :R]), join_columns(proj_stack[:, R:]), join_columns(step_stack), join_columns(conv_w_stack), join_columns(conv_b_stack), join_columns(bias_stack), join_columns(decay_stack), join_columns(skip_stack))
```

```python
import functools

import jax
import jax.numpy as jnp
from jax import lax
from jax.experimental import pallas as pl
from jax.experimental.pallas import tpu as pltpu
from jax.sharding import PartitionSpec as P

LANE = 128
ROWS = 16
LOG2E = 1.4426950408889634
F32 = jnp.float32
BF16 = jnp.bfloat16
MESH = pl.DeviceIdType.MESH


def silu_slope(values):
    sigma = jax.nn.sigmoid(values)
    return sigma * (1.0 + values * (1.0 - sigma))


def dot(a, b, over_a, over_b):
    return lax.dot_general(
        a, b, (((over_a,), (over_b,)), ((), ())), preferred_element_type=F32
    )


def kernel(sizes, *refs):
    Z, Y, T, C, R, N, K = sizes
    CB = C // LANE
    nz = N // Z
    cr = 2 * N // Y
    rz = R // Z
    L = Z // 2
    M = Z - 1 - L
    nb = T // ROWS
    (
        x_h, gate_h, og_h, cw_h, cb_h, pw_h, sw_h, sb_h, dl_h, sk_h,
        gin_o, ggate_o, gproj_o, gcoef_o, gstep_o, gcw_o, gcb_o, gsb_o, gdl_o, gsk_o,
        x_v, gate_v, og_v, cw_v, cb_v, pw_v, sw_v, sb_v, dl_v, sk_v,
        halo_v, xe_v, slope_v, co_v, cv_v, sbuf, rbuf, gbuf, ct_v, bc_v,
        st_v, sig_v, dr_v, g_v, gg_v, sp_v, stot_v, a2_v, a3_v, f_v, hist_v,
        ebuf, erecv, obuf, pbuf, sin_v, cin_v, so_v, dd_v, ab_v, pre_v, cg_v, dg_v,
        gs_v, gp_v, gc_v, bct_v, dc_v, halo2_v, oth_v, mbuf, mrecv, ag_v,
        lsend, lrecv, msend, mrcv2,
        lsem, hs, hr, h2s, h2r, s1, r1, s2, r2, s3, r3, s4, r4,
        ss_s, ss_r, se_s, se_r, sp_s, sp_r, sm_s, sm_r, sg_s, sg_r,
        ls_s, ls_r, ms_s, ms_r,
    ) = refs
    z = lax.axis_index("ctx")
    c = lax.axis_index("chan")
    nxt = lax.rem(z + 1, Z)
    prv = lax.rem(z + Z - 1, Z)

    def remote(src, dst, send, recv, device):
        return pltpu.make_async_remote_copy(
            src_ref=src, dst_ref=dst, send_sem=send, recv_sem=recv,
            device_id=device, device_id_type=MESH,
        )

    def settle(ref, sem):
        pltpu.make_async_copy(ref, ref, sem).wait()

    def to_peers(axis, count, me, src_of, dst, send, recv):
        @pl.loop(1, count)
        def _(k):
            peer = lax.rem(me + k, count)
            remote(src_of(peer), dst, send, recv, {axis: peer}).start()

    pairs = (
        (x_h, x_v), (cw_h, cw_v), (cb_h, cb_v), (pw_h, pw_v), (gate_h, gate_v),
        (og_h, og_v), (sw_h, sw_v), (sb_h, sb_v), (dl_h, dl_v), (sk_h, sk_v),
    )
    loads = [pltpu.make_async_copy(a, b, lsem.at[i]) for i, (a, b) in enumerate(pairs)]
    for load in loads:
        load.start()
    barrier = pltpu.get_barrier_semaphore()

    @pl.loop(1, Z)
    def _(k):
        pl.semaphore_signal(
            barrier, inc=1, device_id={"ctx": lax.rem(z + k, Z)}, device_id_type=MESH
        )

    @pl.loop(1, Y)
    def _(k):
        pl.semaphore_signal(
            barrier, inc=1, device_id={"chan": lax.rem(c + k, Y)}, device_id_type=MESH
        )

    for load in loads[:4]:
        load.wait()
    pl.semaphore_wait(barrier, Z - 1 + Y - 1)

    halo = remote(x_v.at[pl.ds(T - ROWS, ROWS)], halo_v, hs, hr, {"ctx": nxt})
    halo.start()
    xe_v[ROWS:, :] = x_v[...].astype(F32)
    halo.wait_recv()
    xe_v[0:ROWS, :] = jnp.where(z == 0, 0.0, halo_v[...].astype(F32))

    @pl.loop(0, nb)
    def _(b):
        base = pl.multiple_of(b * ROWS, ROWS)
        window = xe_v[pl.ds(base, 2 * ROWS), :]
        pre = jnp.broadcast_to(cb_v[...], (ROWS, C))
        for k in range(K):
            first = ROWS - (K - 1) + k
            pre = pre + cw_v[k : k + 1, :] * window[first : first + ROWS]
        sigma = jax.nn.sigmoid(pre)
        out = (pre * sigma).astype(BF16)
        co_v[pl.ds(base, ROWS), :] = out
        cv_v[pl.ds(base, ROWS), :] = out.astype(F32)
        slope_v[pl.ds(base, ROWS), :] = sigma * (1.0 + pre * (1.0 - sigma))

    def pack(product, coefs):
        for d in range(Y):
            sbuf[d, 0:ROWS, :] = product[ROWS * d : ROWS * (d + 1)].astype(BF16)
            row = coefs[cr * d : cr * (d + 1)]
            if cr == 1:
                row = jnp.broadcast_to(row, (ROWS, LANE))
            else:
                row = jnp.concatenate([row] * (ROWS // cr), axis=0)
            sbuf[d, ROWS : 2 * ROWS, :] = row.astype(BF16)
        rbuf[c] = sbuf[c]

    def scatter_start(send, recv):
        to_peers("chan", Y, c, lambda d: sbuf.at[d], rbuf.at[c], send, recv)

    def reduce_and_spread(send, recv, gsend, grecv):
        settle(rbuf.at[pl.ds(0, Y - 1)], recv)
        total = lax.fori_loop(
            0, Y, lambda s, a: a + rbuf[s].astype(F32), jnp.zeros((2 * ROWS, LANE), F32),
            unroll=4,
        )
        gbuf[c] = total.astype(BF16)
        to_peers("chan", Y, c, lambda d: gbuf.at[c], gbuf.at[c], gsend, grecv)
        settle(sbuf.at[pl.ds(0, Y - 1)], send)

    def spread_finish(gsend, grecv):
        settle(gbuf.at[pl.ds(0, Y - 1)], grecv)
        for d in range(Y):
            rows = gbuf[d, ROWS : 2 * ROWS, :].astype(F32)
            ct_v[cr * d : cr * (d + 1), :] = rows[0:cr]
        settle(gbuf.at[pl.ds(0, Y - 1)], gsend)

    pack(
        dot(pw_v[0:R, :], co_v[...], 1, 1),
        dot(pw_v[R : R + 2 * N, :], co_v[...], 1, 1),
    )
    scatter_start(s1, r1)

    for load in loads[4:]:
        load.wait()

    @pl.loop(0, nb)
    def _(b):
        rows = pl.ds(pl.multiple_of(b * ROWS, ROWS), ROWS)
        gate = gate_v[rows, :].astype(F32)
        grad = og_v[rows, :].astype(F32)
        sigma = jax.nn.sigmoid(gate)
        g_v[rows, :] = grad * (gate * sigma)
        gg_v[rows, :] = grad * (sigma * (1.0 + gate * (1.0 - sigma)))

    a2 = -jnp.exp(dl_v[...])
    a2_v[...] = a2
    for n in range(N):
        for l in range(CB):
            a3_v[n, l : l + 1, :] = a2[n : n + 1, LANE * l : LANE * (l + 1)] * LOG2E

    reduce_and_spread(s1, r1, s2, r2)
    spread_finish(s2, r2)

    slt = gbuf[:, 0:ROWS, :].reshape(R, T)
    sp_v[...] = dot(slt, sw_v[...], 0, 0)

    def sizes_block(b, carry):
        size_sum, skip_sum = carry
        rows = pl.ds(pl.multiple_of(b * ROWS, ROWS), ROWS)
        pre = sp_v[rows, :] + sb_v[...]
        size = jnp.maximum(pre, 0.0) + jnp.log1p(jnp.exp(-jnp.abs(pre)))
        st_v[rows, :] = size
        sig_v[rows, :] = jax.nn.sigmoid(pre)
        conv = cv_v[rows, :]
        dr_v[rows, :] = size * conv
        size_sum = size_sum + jnp.sum(size, axis=0, keepdims=True)
        skip_sum = skip_sum + jnp.sum(g_v[rows, :] * conv, axis=0, keepdims=True)
        return size_sum, skip_sum

    size_sum, skip_sum = lax.fori_loop(
        0, nb, sizes_block, (jnp.zeros((1, C), F32), jnp.zeros((1, C), F32))
    )
    oth_v[...] = jnp.zeros_like(oth_v)
    oth_v[K + 2 : K + 3, :] = skip_sum
    for l in range(CB):
        stot_v[z, l : l + 1, :] = size_sum[:, LANE * l : LANE * (l + 1)]
    to_peers("ctx", Z, z, lambda p: stot_v.at[z], stot_v.at[z], ss_s, ss_r)

    U = 8

    def forward_local(b, h):
        shift = lax.rem(T - b * U, T)
        turned = pltpu.roll(ct_v[...], shift, 1)
        a2s = a2_v[...] * LOG2E
        for i in range(U):
            t = b * U + i
            cols = jnp.broadcast_to(turned[:, i : i + 1], (2 * N, LANE))
            bc_v[t] = cols
            size = st_v[pl.ds(t, 1), :]
            drive = dr_v[pl.ds(t, 1), :]
            f = jnp.exp2(size * a2s)
            f_v[t] = f
            h = f * h + drive * jnp.concatenate([cols[0:N]] * CB, axis=1)
        return h

    end = lax.fori_loop(0, T // U, forward_local, jnp.zeros((N, C), F32))

    def backward_local(b, q):
        for i in range(U):
            t = T - 1 - (b * U + i)
            coef = bc_v[t, N : 2 * N, :]
            q = f_v[t] * (jnp.concatenate([coef] * CB, axis=1) * g_v[pl.ds(t, 1), :] + q)
        return q

    head = lax.fori_loop(0, T // U, backward_local, jnp.zeros((N, C), F32))

    for n in range(N):
        p, i = divmod(n, nz)
        for l in range(CB):
            lanes = slice(LANE * l, LANE * (l + 1))
            ebuf[p, (2 * i) * CB + l : (2 * i) * CB + l + 1, :] = end[n : n + 1, lanes]
            ebuf[p, (2 * i + 1) * CB + l : (2 * i + 1) * CB + l + 1, :] = head[n : n + 1, lanes]
    erecv[z] = ebuf[z]
    to_peers("ctx", Z, z, lambda p: ebuf.at[p], erecv.at[z], se_s, se_r)
    settle(stot_v.at[pl.ds(0, Z - 1)], ss_r)
    settle(stot_v.at[pl.ds(0, Z - 1)], ss_s)
    decays = []
    for i in range(nz):
        rate = a3_v[z * nz + i][0:CB]
        decays.append([jnp.exp2(rate * stot_v[d][0:CB]) for d in range(Z)])
    settle(erecv.at[pl.ds(0, Z - 1)], se_r)
    for i in range(nz):
        top = slice(2 * i * CB, (2 * i + 1) * CB)
        low = slice((2 * i + 1) * CB, (2 * i + 2) * CB)
        state = jnp.zeros((CB, LANE), F32)
        for d in range(Z):
            obuf[d, top, :] = state
            state = erecv[d, top, :] + decays[i][d] * state
        state = jnp.zeros((CB, LANE), F32)
        for d in reversed(range(Z)):
            obuf[d, low, :] = state
            state = erecv[d, low, :] + decays[i][d] * state
    pbuf[z] = obuf[z]
    to_peers("ctx", Z, z, lambda p: obuf.at[p], pbuf.at[z], sp_s, sp_r)
    settle(ebuf.at[pl.ds(0, Z - 1)], se_s)
    settle(pbuf.at[pl.ds(0, Z - 1)], sp_r)
    for n in range(N):
        p, i = divmod(n, nz)
        for l in range(CB):
            lanes = slice(LANE * l, LANE * (l + 1))
            sin_v[n : n + 1, lanes] = pbuf[p, (2 * i) * CB + l : (2 * i) * CB + l + 1, :]
            cin_v[n : n + 1, lanes] = pbuf[p, (2 * i + 1) * CB + l : (2 * i + 1) * CB + l + 1, :]
    settle(obuf.at[pl.ds(0, Z - 1)], sp_s)

    lane = lax.broadcasted_iota(jnp.int32, (N, LANE), 1)

    def fold(wide):
        total = wide[:, 0:LANE]
        for l in range(1, CB):
            total = total + wide[:, LANE * l : LANE * (l + 1)]
        return jnp.sum(total, axis=1, keepdims=True)

    def forward_pass(b, carry):
        h, acc = carry
        for i in range(U):
            t = b * U + i
            cols = bc_v[t]
            drive = dr_v[pl.ds(t, 1), :]
            hist_v[t] = h
            h = f_v[t] * h + drive * jnp.concatenate([cols[0:N]] * CB, axis=1)
            out = jnp.concatenate([cols[N : 2 * N]] * CB, axis=1) * h
            so_v[pl.ds(t, 1), :] = jnp.sum(out, axis=0, keepdims=True)
            acc = jnp.where(lane == t, fold(h * g_v[pl.ds(t, 1), :]), acc)
        return h, acc

    _, coef_out = lax.fori_loop(
        0, T // U, forward_pass, (sin_v[...], jnp.zeros((N, LANE), F32))
    )

    def backward_pass(b, carry):
        q, acc, decay = carry
        a2w = a2_v[...]
        for i in range(U):
            t = T - 1 - (b * U + i)
            cols = bc_v[t]
            g = g_v[pl.ds(t, 1), :]
            adj = jnp.concatenate([cols[N : 2 * N]] * CB, axis=1) * g + q
            q = f_v[t] * adj
            w = q * hist_v[t]
            dd_v[pl.ds(t, 1), :] = jnp.sum(a2w * w, axis=0, keepdims=True)
            ab = jnp.concatenate([cols[0:N]] * CB, axis=1) * adj
            ab_v[pl.ds(t, 1), :] = jnp.sum(ab, axis=0, keepdims=True)
            decay = decay + w * st_v[pl.ds(t, 1), :]
            acc = jnp.where(lane == t, fold(adj * dr_v[pl.ds(t, 1), :]), acc)
        return q, acc, decay

    _, coef_in, decay = lax.fori_loop(
        0, T // U, backward_pass,
        (cin_v[...], jnp.zeros((N, LANE), F32), jnp.zeros((N, C), F32)),
    )
    dg_v[...] = decay * a2_v[...]

    def gate_block(b, bias_sum):
        rows = pl.ds(pl.multiple_of(b * ROWS, ROWS), ROWS)
        conv = cv_v[rows, :]
        g = g_v[rows, :]
        ab = ab_v[rows, :]
        skip = sk_v[...]
        pre = (dd_v[rows, :] + ab * conv) * sig_v[rows, :]
        pre_v[rows, :] = pre.astype(BF16)
        ggate_o[rows, :] = (gg_v[rows, :] * (so_v[rows, :] + skip * conv)).astype(BF16)
        cg_v[rows, :] = ab * st_v[rows, :] + skip * g
        return bias_sum + jnp.sum(pre, axis=0, keepdims=True)

    oth_v[K + 1 : K + 2, :] = lax.fori_loop(0, nb, gate_block, jnp.zeros((1, C), F32))

    pack(
        dot(sw_v[...], pre_v[...], 1, 1),
        jnp.concatenate([coef_in, coef_out], axis=0),
    )
    slt2 = gbuf[:, 0:ROWS, :].reshape(R, T)
    gs_v[...] = dot(slt2, pre_v[...], 1, 0).reshape(Z, rz, C)
    scatter_start(s3, r3)

    def ring(which, part, s):
        left, right = {"ctx": prv}, {"ctx": nxt}
        if s < L:
            value = part[lax.rem(z + Z - L + s, Z)]
            if s:
                settle(lrecv.at[which, s - 1], ls_r.at[which, s - 1])
                value = value + lrecv[which, s - 1].astype(F32)
            lsend[which, s] = value.astype(BF16)
            remote(
                lsend.at[which, s], lrecv.at[which, s],
                ls_s.at[which, s], ls_r.at[which, s], left,
            ).start()
        if s < M:
            value = part[lax.rem(z + M - s, Z)]
            if s:
                settle(mrcv2.at[which, s - 1], ms_r.at[which, s - 1])
                value = value + mrcv2[which, s - 1].astype(F32)
            msend[which, s] = value.astype(BF16)
            remote(
                msend.at[which, s], mrcv2.at[which, s],
                ms_s.at[which, s], ms_r.at[which, s], right,
            ).start()

    def ring_end(which, part):
        value = part[z]
        settle(lrecv.at[which, L - 1], ls_r.at[which, L - 1])
        value = value + lrecv[which, L - 1].astype(F32)
        if M:
            settle(mrcv2.at[which, M - 1], ms_r.at[which, M - 1])
            value = value + mrcv2[which, M - 1].astype(F32)
        for s in range(L):
            settle(lsend.at[which, s], ls_s.at[which, s])
        for s in range(M):
            settle(msend.at[which, s], ms_s.at[which, s])
        return value

    ring(0, gs_v, 0)
    ring(0, gs_v, 1)
    reduce_and_spread(s3, r3, s4, r4)
    ring(0, gs_v, 2)
    ring(0, gs_v, 3)
    spread_finish(s4, r4)

    bpt = gbuf[:, 0:ROWS, :].reshape(R, T)
    bct_v[...] = ct_v[...].astype(BF16)
    gp_v[...] = dot(bpt, co_v[...], 1, 0).reshape(Z, rz, C)
    ring(1, gp_v, 0)
    sp_v[...] = dot(bpt, pw_v[0:R, :], 0, 0) + dot(bct_v[...], pw_v[R : R + 2 * N, :], 0, 0)

    def conv_block(b, carry):
        base = pl.multiple_of(b * ROWS, ROWS)
        rows = pl.ds(base, ROWS)
        grad = (cg_v[rows, :] + sp_v[rows, :]) * slope_v[rows, :]
        dc_v[rows, :] = grad
        window = xe_v[pl.ds(base, 2 * ROWS), :]
        new = []
        for k in range(K):
            first = ROWS - (K - 1) + k
            taps = grad * window[first : first + ROWS]
            new.append(carry[k] + jnp.sum(taps, axis=0, keepdims=True))
        new.append(carry[K] + jnp.sum(grad, axis=0, keepdims=True))
        return tuple(new)

    sums = lax.fori_loop(0, nb, conv_block, (jnp.zeros((1, C), F32),) * (K + 1))
    halo2 = remote(dc_v.at[pl.ds(0, 8)], halo2_v, h2s, h2r, {"ctx": prv})
    halo2.start()
    for k in range(K + 1):
        oth_v[k : k + 1, :] = sums[k]
    gc_v[...] = dot(bct_v[...], co_v[...], 1, 0)
    ring(0, gs_v, 4)
    ring(1, gp_v, 1)

    other = 8 * CB // Z
    coef = 2 * N // Z
    for p in range(Z):
        at = 0
        for i in range(nz):
            for l in range(CB):
                n = p * nz + i
                mbuf[p, at : at + 1, :] = dg_v[n : n + 1, LANE * l : LANE * (l + 1)]
                at += 1
        for i in range(other):
            j, l = divmod(p * other + i, CB)
            mbuf[p, at : at + 1, :] = oth_v[j : j + 1, LANE * l : LANE * (l + 1)]
            at += 1
        for i in range(coef):
            for l in range(CB):
                n = p * coef + i
                mbuf[p, at : at + 1, :] = gc_v[n : n + 1, LANE * l : LANE * (l + 1)]
                at += 1
    mrecv[z] = mbuf[z]
    to_peers("ctx", Z, z, lambda p: mbuf.at[p], mrecv.at[z], sm_s, sm_r)

    halo2.wait_recv()
    dc_v[pl.ds(T, 8), :] = jnp.where(z == Z - 1, 0.0, halo2_v[...])

    @pl.loop(0, nb)
    def _(b):
        base = pl.multiple_of(b * ROWS, ROWS)
        window = dc_v[pl.ds(base, ROWS + 8), :]
        total = jnp.zeros((ROWS, C), F32)
        for k in range(K):
            lead = K - 1 - k
            total = total + cw_v[k : k + 1, :] * window[lead : lead + ROWS]
        gin_o[pl.ds(base, ROWS), :] = total.astype(BF16)

    ring(0, gs_v, 5)
    ring(1, gp_v, 2)
    settle(mrecv.at[pl.ds(0, Z - 1)], sm_r)
    total = mrecv[0]
    for d in range(1, Z):
        total = total + mrecv[d]
    shared = nz * CB + other
    ag_v[z] = total[0 : ag_v.shape[1]]
    to_peers("ctx", Z, z, lambda p: ag_v.at[z], ag_v.at[z], sg_s, sg_r)
    for i in range(coef):
        for l in range(CB):
            row = shared + i * CB + l
            gcoef_o[i : i + 1, LANE * l : LANE * (l + 1)] = total[row : row + 1]
    ring(0, gs_v, 6)
    ring(1, gp_v, 3)
    ring(0, gs_v, 7)
    ring(1, gp_v, 4)
    gstep_o[...] = ring_end(0, gs_v)
    ring(1, gp_v, 5)
    settle(ag_v.at[pl.ds(0, Z - 1)], sg_r)
    outs = [gcw_o.at[k : k + 1] for k in range(K)] + [gcb_o, gsb_o, gsk_o]
    for p in range(Z):
        at = 0
        for i in range(nz):
            for l in range(CB):
                n = p * nz + i
                gdl_o[n : n + 1, LANE * l : LANE * (l + 1)] = ag_v[p, at : at + 1, :]
                at += 1
        for i in range(other):
            j, l = divmod(p * other + i, CB)
            if j < len(outs):
                outs[j][:, LANE * l : LANE * (l + 1)] = ag_v[p, at : at + 1, :]
            at += 1
    ring(1, gp_v, 6)
    ring(1, gp_v, 7)
    gproj_o[...] = ring_end(1, gp_v)
    halo.wait_send()
    halo2.wait_send()
    settle(mbuf.at[pl.ds(0, Z - 1)], sm_s)
    settle(ag_v.at[pl.ds(0, Z - 1)], sg_s)


def body(sizes, *args):
    Z, Y, T, C, R, N, K = sizes
    conv_input, gate, og, cw, cb, pw, sw, sb, dl, sk = args
    CB = C // LANE
    nz = N // Z
    rz = R // Z
    L = Z // 2
    M = max(Z - 1 - L, 1)
    coef = 2 * N // Z
    other = 8 * CB // Z
    er = 2 * nz * CB
    small = -(-(nz * CB + other + coef * CB) // 8) * 8
    back = -(-(nz * CB + other) // 8) * 8
    vm = pltpu.VMEM
    dma = pltpu.SemaphoreType.DMA
    scratch = [
        vm((T, C), BF16), vm((T, C), BF16), vm((T, C), BF16), vm((K, C), F32), vm((1, C), F32),
        vm((R + 2 * N, C), BF16), vm((R, C), BF16), vm((1, C), F32), vm((N, C), F32), vm((1, C), F32),
        vm((ROWS, C), BF16), vm((T + ROWS, C), F32), vm((T, C), F32), vm((T, C), BF16), vm((T, C), F32),
        vm((Y, 2 * ROWS, LANE), BF16), vm((Y, 2 * ROWS, LANE), BF16), vm((Y, 2 * ROWS, LANE), BF16),
        vm((2 * N, T), F32), vm((T, 2 * N, LANE), F32),
        *[vm((T, C), F32) for _ in range(6)],
        vm((Z, 8, LANE), F32), vm((N, C), F32), vm((N, 8, LANE), F32), vm((T, N, C), F32), vm((T, N, C), F32),
        *[vm((Z, er, LANE), F32) for _ in range(4)], vm((N, C), F32), vm((N, C), F32),
        vm((T, C), F32), vm((T, C), F32), vm((T, C), F32), vm((T, C), BF16), vm((T, C), F32), vm((N, C), F32),
        vm((Z, rz, C), F32), vm((Z, rz, C), F32), vm((2 * N, C), F32), vm((2 * N, T), BF16),
        vm((T + 8, C), F32), vm((8, C), F32), vm((8, C), F32),
        vm((Z, small, LANE), F32), vm((Z, small, LANE), F32), vm((Z, back, LANE), F32),
        vm((2, L, rz, C), BF16), vm((2, L, rz, C), BF16), vm((2, M, rz, C), BF16), vm((2, M, rz, C), BF16),
        dma((10,)), *[dma(()) for _ in range(22)],
        dma((2, L)), dma((2, L)), dma((2, M)), dma((2, M)),
    ]
    shape = jax.ShapeDtypeStruct
    outs = pl.pallas_call(
        functools.partial(kernel, sizes),
        out_shape=[
            shape((T, C), BF16), shape((T, C), BF16), shape((rz, C), F32), shape((coef, C), F32),
            shape((rz, C), F32), shape((K, C), F32), shape((1, C), F32), shape((1, C), F32),
            shape((N, C), F32), shape((1, C), F32),
        ],
        in_specs=[pl.BlockSpec(memory_space=pl.ANY)] * 10,
        out_specs=[pl.BlockSpec(memory_space=pltpu.VMEM)] * 10,
        scratch_shapes=scratch,
        compiler_params=pltpu.CompilerParams(
            collective_id=0, has_side_effects=True, vmem_limit_bytes=48 * 2**20
        ),
    )(conv_input, gate, og, cw, cb[None], pw, sw, sb[None], dl, sk[None])
    flat = lambda a: a.reshape(-1)
    return (*outs[:6], flat(outs[6]), flat(outs[7]), outs[8], flat(outs[9]))


def solution(mesh):
    Z, Y = mesh.shape["ctx"], mesh.shape["chan"]

    def run(conv_input, *rest):
        cw, pw, sw, dl = rest[2], rest[4], rest[5], rest[7]
        sizes = (
            Z, Y, conv_input.shape[0] // Z, conv_input.shape[1] // Y,
            sw.shape[0], dl.shape[0], cw.shape[0],
        )
        return jax.shard_map(
            functools.partial(body, sizes), mesh=mesh, in_specs=in_specs, out_specs=out_specs,
            check_vma=False,
        )(conv_input, *rest)

    both, wide, flat = P("ctx", "chan"), P(None, "chan"), P("chan")
    in_specs = (both, both, both, wide, flat, wide, wide, flat, wide, flat)
    out_specs = (both, both, both, both, both, wide, flat, flat, wide, flat)
    return run
```

```python
import functools

import jax
import jax.numpy as jnp
from jax import lax
from jax.experimental import pallas as pl
from jax.experimental.pallas import tpu as pltpu
from jax.sharding import PartitionSpec as P

LANE = 128
ROWS = 16
LOG2E = 1.4426950408889634
VMEM_BYTES = 60 * 2**20
F32 = jnp.float32
BF16 = jnp.bfloat16
MESH = pl.DeviceIdType.MESH


def silu_slope(values):
    sigma = jax.nn.sigmoid(values)
    return sigma * (1.0 + values * (1.0 - sigma))


def dot(a, b, over_a, over_b):
    return lax.dot_general(
        a, b, (((over_a,), (over_b,)), ((), ())), preferred_element_type=F32
    )


def kernel(sizes, *refs):
    Z, Y, T, C, R, N, K = sizes
    CB = C // LANE
    nz = N // Z
    Q = Y // 2
    coef = 2 * N // Z
    rz = R // Z
    L = Z // 2
    M = Z - 1 - L
    nb = T // ROWS
    (
        x_h, gate_h, og_h, cw_h, cb_h, pw_h, sw_h, sb_h, dl_h, sk_h,
        gin_h, ggate_h, gproj_h, gcoef_h, gstep_h, gcw_h, gcb_h, gsb_h, gdl_h, gsk_h,
        gin_o, ggate_o, gproj_o, gcoef_o, gstep_o, gcw_o, gcb_o, gsb_o, gdl_o, gsk_o,
        x_v, gate_v, og_v, cw_v, cb_v, pw_v, sw_v, sb_v, dl_v, sk_v,
        halo_v, xe_v, slope_v, co_v, cv_v, sbuf, hbuf, tbuf, rbuf, gbuf, slt_v, ct_v, bc_v,
        st_v, sig_v, dr_v, g_v, gg_v, sp_v, stot_v, dec_v, a2_v, a3_v, f_v, hist_v,
        es_v, er_v, eo_v, ep_v, hs_v, hr_v, ho_v, hp_v, sin_v, cin_v,
        so_v, dd_v, ab_v, pre_v, cg_v, dg_v,
        gs_v, gp_v, gc_v, dc_v, halo2_v, oth_v, mf_v, mbuf, mrecv, ag_v, lsend, lrecv, msend, mrcv2,
        lsem, osem, hs, hr, h2s, h2r, ss_s, ss_r, es_s, es_r, ep_s, ep_r, hs_s, hs_r, hp_s, hp_r,
        sm_s, sm_r, sg_s, sg_r, send_sums, recv_sums, ls_s, ls_r, ms_s, ms_r,
    ) = refs
    outs_v = (gin_o, ggate_o, gproj_o, gcoef_o, gstep_o, gcw_o, gcb_o, gsb_o, gdl_o, gsk_o)
    outs_h = (gin_h, ggate_h, gproj_h, gcoef_h, gstep_h, gcw_h, gcb_h, gsb_h, gdl_h, gsk_h)
    z = lax.axis_index("ctx")
    c = lax.axis_index("chan")
    core = lax.rem(c, 2)
    chip = lax.div(c, 2)
    sibling = c + 1 - 2 * core
    nxt = lax.rem(z + 1, Z)
    prv = lax.rem(z + Z - 1, Z)

    def remote(src, dst, send, recv, device):
        return pltpu.make_async_remote_copy(
            src_ref=src, dst_ref=dst, send_sem=send, recv_sem=recv,
            device_id=device, device_id_type=MESH,
        )

    def settle(ref, sem):
        pltpu.make_async_copy(ref, ref, sem).wait()

    def to_ctx(src_of, dst, send, recv):
        @pl.loop(1, Z)
        def _(k):
            peer = lax.rem(z + k, Z)
            remote(src_of(peer), dst, send, recv, {"ctx": peer}).start()

    def lanes(l):
        return slice(LANE * l, LANE * (l + 1))

    def store(i):
        pltpu.make_async_copy(outs_v[i], outs_h[i], osem.at[i]).start()

    pairs = (
        (x_h, x_v), (cw_h, cw_v), (cb_h, cb_v), (pw_h, pw_v), (gate_h, gate_v),
        (og_h, og_v), (sw_h, sw_v), (sb_h, sb_v), (dl_h, dl_v), (sk_h, sk_v),
    )
    loads = [pltpu.make_async_copy(a, b, lsem.at[i]) for i, (a, b) in enumerate(pairs)]
    for load in loads:
        load.start()
    barrier = pltpu.get_barrier_semaphore()

    @pl.loop(1, Z)
    def _(k):
        pl.semaphore_signal(
            barrier, inc=1, device_id={"ctx": lax.rem(z + k, Z)}, device_id_type=MESH
        )

    @pl.loop(1, Q)
    def _(k):
        pl.semaphore_signal(
            barrier, inc=1, device_id={"chan": 2 * lax.rem(chip + k, Q) + core}, device_id_type=MESH
        )

    pl.semaphore_signal(barrier, inc=1, device_id={"chan": sibling}, device_id_type=MESH)
    for load in loads[:4]:
        load.wait()
    pl.semaphore_wait(barrier, Z + Q - 1)

    halo = remote(x_v.at[pl.ds(T - ROWS, ROWS)], halo_v, hs, hr, {"ctx": nxt})
    halo.start()
    xe_v[ROWS:, :] = x_v[...].astype(F32)
    halo.wait_recv()
    xe_v[0:ROWS, :] = jnp.where(z == 0, 0.0, halo_v[...].astype(F32))

    @pl.loop(0, nb)
    def _(b):
        base = pl.multiple_of(b * ROWS, ROWS)
        window = xe_v[pl.ds(base, 2 * ROWS), :]
        pre = jnp.broadcast_to(cb_v[...], (ROWS, C))
        for k in range(K):
            first = ROWS - (K - 1) + k
            pre = pre + cw_v[k : k + 1, :] * window[first : first + ROWS]
        sigma = jax.nn.sigmoid(pre)
        out = (pre * sigma).astype(BF16)
        co_v[pl.ds(base, ROWS), :] = out
        cv_v[pl.ds(base, ROWS), :] = out.astype(F32)
        slope_v[pl.ds(base, ROWS), :] = sigma * (1.0 + pre * (1.0 - sigma))

    half = Q + 1
    mine = core * half
    at_chip = chip + jnp.where(chip > 0, 1, 0)

    def either(when, yes, no):
        pl.when(when)(yes)
        pl.when(jnp.logical_not(when))(no)

    def to_sibling(which):
        remote(
            sbuf.at[pl.ds((1 - core) * half, half)], hbuf,
            send_sums.at[which, 0], recv_sums.at[which, 0], {"chan": sibling},
        ).start()

    def scatter(which):
        settle(hbuf, recv_sums.at[which, 0])
        settle(hbuf, send_sums.at[which, 0])
        both = sbuf[pl.ds(mine, half)].astype(F32) + hbuf[...].astype(F32)
        tbuf[...] = both.astype(BF16)
        send, recv = send_sums.at[which, 1], recv_sums.at[which, 1]

        @pl.loop(1, Q)
        def _(k):
            peer = lax.rem(chip + k, Q)
            device = {"chan": 2 * peer + core}

            def two():
                remote(tbuf.at[pl.ds(0, 2)], rbuf.at[chip], send, recv, device).start()

            def one():
                remote(
                    tbuf.at[pl.ds(peer + 1, 1)], rbuf.at[chip, pl.ds(0, 1)], send, recv, device
                ).start()

            either(peer == 0, two, one)

        rbuf[chip, 0] = tbuf[at_chip]
        rbuf[chip, 1] = tbuf[1]

    def spread(which):
        send, recv = send_sums.at[which, 2], recv_sums.at[which, 2]

        def part(j):
            total = rbuf[0, j].astype(F32)
            for s in range(1, Q):
                total = total + rbuf[s, j].astype(F32)
            return total.astype(BF16)

        def out(block):
            @pl.loop(1, Q)
            def _(k):
                device = {"chan": 2 * lax.rem(chip + k, Q) + core}
                remote(block, block, send, recv, device).start()

        def two():
            settle(rbuf.at[pl.ds(0, Q - 1)], recv_sums.at[which, 1])
            gbuf[mine] = part(0)
            gbuf[mine + 1] = part(1)
            out(gbuf.at[pl.ds(mine, 2)])
            settle(tbuf.at[pl.ds(0, Q - 1)], send_sums.at[which, 1])

        def one():
            settle(rbuf.at[pl.ds(0, Q - 1), pl.ds(0, 1)], recv_sums.at[which, 1])
            gbuf[mine + at_chip] = part(0)
            out(gbuf.at[pl.ds(mine + at_chip, 1)])
            settle(tbuf.at[pl.ds(0, Q)], send_sums.at[which, 1])

        either(chip == 0, two, one)

    def share(which):
        either(
            chip == 0,
            lambda: settle(tbuf.at[pl.ds(0, Q - 1)], recv_sums.at[which, 2]),
            lambda: settle(tbuf.at[pl.ds(0, Q)], recv_sums.at[which, 2]),
        )
        block = gbuf.at[pl.ds(mine, half)]
        remote(
            block, block, send_sums.at[which, 3], recv_sums.at[which, 3], {"chan": sibling}
        ).start()

    def shared(which):
        settle(hbuf, recv_sums.at[which, 3])

    def sums_settle(which):
        either(
            chip == 0,
            lambda: settle(rbuf.at[pl.ds(0, Q - 1)], send_sums.at[which, 2]),
            lambda: settle(rbuf.at[pl.ds(0, Q - 1), pl.ds(0, 1)], send_sums.at[which, 2]),
        )
        settle(hbuf, send_sums.at[which, 3])

    sbuf[...] = dot(pw_v[...], co_v[...], 1, 1).astype(BF16).reshape(Y + 2, ROWS, LANE)
    to_sibling(0)

    for load in loads[4:]:
        load.wait()

    scatter(0)

    @pl.loop(0, nb)
    def _(b):
        rows = pl.ds(pl.multiple_of(b * ROWS, ROWS), ROWS)
        gate = gate_v[rows, :].astype(F32)
        grad = og_v[rows, :].astype(F32)
        sigma = jax.nn.sigmoid(gate)
        g_v[rows, :] = grad * (gate * sigma)
        gg_v[rows, :] = grad * (sigma * (1.0 + gate * (1.0 - sigma)))

    a2 = -jnp.exp(dl_v[...])
    a2_v[...] = a2
    for n in range(N):
        for l in range(CB):
            a3_v[n, l : l + 1, :] = a2[n : n + 1, LANE * l : LANE * (l + 1)] * LOG2E

    spread(0)
    share(0)
    shared(0)
    total = gbuf[...].reshape(R + 2 * N, T)
    slt_v[...] = total[0:R]
    ct_v[...] = total[R:].astype(F32)
    sp_v[...] = dot(total[0:R], sw_v[...], 0, 0)

    def sizes_block(b, carry):
        size_sum, skip_sum = carry
        rows = pl.ds(pl.multiple_of(b * ROWS, ROWS), ROWS)
        pre = sp_v[rows, :] + sb_v[...]
        size = jnp.maximum(pre, 0.0) + jnp.log1p(jnp.exp(-jnp.abs(pre)))
        st_v[rows, :] = size
        sig_v[rows, :] = jax.nn.sigmoid(pre)
        conv = cv_v[rows, :]
        dr_v[rows, :] = size * conv
        size_sum = size_sum + jnp.sum(size, axis=0, keepdims=True)
        skip_sum = skip_sum + jnp.sum(g_v[rows, :] * conv, axis=0, keepdims=True)
        return size_sum, skip_sum

    size_sum, skip_sum = lax.fori_loop(
        0, nb, sizes_block, (jnp.zeros((1, C), F32), jnp.zeros((1, C), F32))
    )
    sums_settle(0)
    oth_v[...] = jnp.zeros_like(oth_v)
    oth_v[K + 2 : K + 3, :] = skip_sum
    for l in range(CB):
        stot_v[z, l : l + 1, :] = size_sum[:, LANE * l : LANE * (l + 1)]
    to_ctx(lambda p: stot_v.at[z], stot_v.at[z], ss_s, ss_r)

    U = 8

    def forward_local(b, h):
        shift = lax.rem(T - b * U, T)
        turned = pltpu.roll(ct_v[...], shift, 1)
        a2s = a2_v[...] * LOG2E
        for i in range(U):
            t = b * U + i
            cols = jnp.broadcast_to(turned[:, i : i + 1], (2 * N, LANE))
            bc_v[t] = cols
            size = st_v[pl.ds(t, 1), :]
            drive = dr_v[pl.ds(t, 1), :]
            f = jnp.exp2(size * a2s)
            f_v[t] = f
            h = f * h + drive * jnp.concatenate([cols[0:N]] * CB, axis=1)
        return h

    end = lax.fori_loop(0, T // U, forward_local, jnp.zeros((N, C), F32))

    def rows_out(values, buf, recv_buf, send, recv):
        for n in range(N):
            p, i = divmod(n, nz)
            for l in range(CB):
                buf[p, i * CB + l : i * CB + l + 1, :] = values[n : n + 1, lanes(l)]
        recv_buf[z] = buf[z]
        to_ctx(lambda p: buf.at[p], recv_buf.at[z], send, recv)

    def rows_combine(recv_buf, out, back, order, recv, send, answer):
        settle(recv_buf.at[pl.ds(0, Z - 1)], recv)
        state = jnp.zeros((nz * CB, LANE), F32)
        for d in order:
            out[d] = state
            state = recv_buf[d] + dec_v[d] * state
        back[z] = out[z]
        to_ctx(lambda p: out.at[p], back.at[z], send, answer)

    def rows_in(back, into, recv):
        settle(back.at[pl.ds(0, Z - 1)], recv)
        for n in range(N):
            p, i = divmod(n, nz)
            for l in range(CB):
                into[n : n + 1, lanes(l)] = back[p, i * CB + l : i * CB + l + 1, :]

    rows_out(end, es_v, er_v, es_s, es_r)

    def backward_local(b, q):
        for i in range(U):
            t = T - 1 - (b * U + i)
            coefs = bc_v[t, N : 2 * N, :]
            q = f_v[t] * (jnp.concatenate([coefs] * CB, axis=1) * g_v[pl.ds(t, 1), :] + q)
        return q

    head = lax.fori_loop(0, T // U, backward_local, jnp.zeros((N, C), F32))
    rows_out(head, hs_v, hr_v, hs_s, hs_r)
    settle(stot_v.at[pl.ds(0, Z - 1)], ss_r)
    for d in range(Z):
        for i in range(nz):
            dec_v[d, i * CB : (i + 1) * CB, :] = jnp.exp2(a3_v[z * nz + i] * stot_v[d])
    rows_combine(er_v, eo_v, ep_v, range(Z), es_r, ep_s, ep_r)
    rows_combine(hr_v, ho_v, hp_v, reversed(range(Z)), hs_r, hp_s, hp_r)
    rows_in(ep_v, sin_v, ep_r)

    lane = lax.broadcasted_iota(jnp.int32, (N, LANE), 1)

    def fold(wide):
        total = wide[:, 0:LANE]
        for l in range(1, CB):
            total = total + wide[:, LANE * l : LANE * (l + 1)]
        return jnp.sum(total, axis=1, keepdims=True)

    def forward_pass(b, carry):
        h, acc = carry
        for i in range(U):
            t = b * U + i
            cols = bc_v[t]
            drive = dr_v[pl.ds(t, 1), :]
            hist_v[t] = h
            h = f_v[t] * h + drive * jnp.concatenate([cols[0:N]] * CB, axis=1)
            out = jnp.concatenate([cols[N : 2 * N]] * CB, axis=1) * h
            so_v[pl.ds(t, 1), :] = jnp.sum(out, axis=0, keepdims=True)
            acc = jnp.where(lane == t, fold(h * g_v[pl.ds(t, 1), :]), acc)
        return h, acc

    _, coef_out = lax.fori_loop(
        0, T // U, forward_pass, (sin_v[...], jnp.zeros((N, LANE), F32))
    )

    rows_in(hp_v, cin_v, hp_r)

    def backward_pass(b, carry):
        q, acc, decay = carry
        a2w = a2_v[...]
        for i in range(U):
            t = T - 1 - (b * U + i)
            cols = bc_v[t]
            g = g_v[pl.ds(t, 1), :]
            adj = jnp.concatenate([cols[N : 2 * N]] * CB, axis=1) * g + q
            q = f_v[t] * adj
            w = q * hist_v[t]
            dd_v[pl.ds(t, 1), :] = jnp.sum(a2w * w, axis=0, keepdims=True)
            ab = jnp.concatenate([cols[0:N]] * CB, axis=1) * adj
            ab_v[pl.ds(t, 1), :] = jnp.sum(ab, axis=0, keepdims=True)
            decay = decay + w * st_v[pl.ds(t, 1), :]
            acc = jnp.where(lane == t, fold(adj * dr_v[pl.ds(t, 1), :]), acc)
        return q, acc, decay

    _, coef_in, decay = lax.fori_loop(
        0, T // U, backward_pass,
        (cin_v[...], jnp.zeros((N, LANE), F32), jnp.zeros((N, C), F32)),
    )
    dg_v[...] = decay * a2_v[...]

    def pre_block(b, bias_sum):
        rows = pl.ds(pl.multiple_of(b * ROWS, ROWS), ROWS)
        pre = (dd_v[rows, :] + ab_v[rows, :] * cv_v[rows, :]) * sig_v[rows, :]
        pre_v[rows, :] = pre.astype(BF16)
        return bias_sum + jnp.sum(pre, axis=0, keepdims=True)

    oth_v[K + 1 : K + 2, :] = lax.fori_loop(0, nb, pre_block, jnp.zeros((1, C), F32))
    back = jnp.concatenate([dot(sw_v[...], pre_v[...], 1, 1), coef_in, coef_out], axis=0)
    sbuf[...] = back.astype(BF16).reshape(Y + 2, ROWS, LANE)
    to_sibling(1)
    gs_v[...] = dot(slt_v[...], pre_v[...], 1, 0).reshape(Z, rz, C)

    def ring(which, part, s):
        left, right = {"ctx": prv}, {"ctx": nxt}
        if s < L:
            value = part[lax.rem(z + Z - L + s, Z)]
            if s:
                settle(lrecv.at[which, s - 1], ls_r.at[which, s - 1])
                value = value + lrecv[which, s - 1].astype(F32)
            lsend[which, s] = value.astype(BF16)
            remote(
                lsend.at[which, s], lrecv.at[which, s],
                ls_s.at[which, s], ls_r.at[which, s], left,
            ).start()
        if s < M:
            value = part[lax.rem(z + M - s, Z)]
            if s:
                settle(mrcv2.at[which, s - 1], ms_r.at[which, s - 1])
                value = value + mrcv2[which, s - 1].astype(F32)
            msend[which, s] = value.astype(BF16)
            remote(
                msend.at[which, s], mrcv2.at[which, s],
                ms_s.at[which, s], ms_r.at[which, s], right,
            ).start()

    def ring_end(which, part):
        value = part[z]
        settle(lrecv.at[which, L - 1], ls_r.at[which, L - 1])
        value = value + lrecv[which, L - 1].astype(F32)
        if M:
            settle(mrcv2.at[which, M - 1], ms_r.at[which, M - 1])
            value = value + mrcv2[which, M - 1].astype(F32)
        for s in range(L):
            settle(lsend.at[which, s], ls_s.at[which, s])
        for s in range(M):
            settle(msend.at[which, s], ms_s.at[which, s])
        return value

    ring(0, gs_v, 0)
    scatter(1)

    @pl.loop(0, nb)
    def _(b):
        rows = pl.ds(pl.multiple_of(b * ROWS, ROWS), ROWS)
        skip = sk_v[...]
        ggate_o[rows, :] = (gg_v[rows, :] * (so_v[rows, :] + skip * cv_v[rows, :])).astype(BF16)
        cg_v[rows, :] = ab_v[rows, :] * st_v[rows, :] + skip * g_v[rows, :]

    store(1)

    other = 8 * CB // Z
    for p in range(Z):
        for i in range(nz):
            for l in range(CB):
                n = p * nz + i
                mf_v[p, i * CB + l : i * CB + l + 1, :] = dg_v[n : n + 1, lanes(l)]
    ring(0, gs_v, 1)
    spread(1)
    ring(0, gs_v, 2)
    share(1)
    ring(0, gs_v, 3)
    shared(1)
    back = gbuf[...].reshape(R + 2 * N, T)
    gp_v[...] = dot(back[0:R], co_v[...], 1, 0).reshape(Z, rz, C)
    ring(1, gp_v, 0)
    sp_v[...] = dot(back, pw_v[...], 0, 0)

    def conv_block(b, carry):
        base = pl.multiple_of(b * ROWS, ROWS)
        rows = pl.ds(base, ROWS)
        grad = (cg_v[rows, :] + sp_v[rows, :]) * slope_v[rows, :]
        dc_v[rows, :] = grad
        window = xe_v[pl.ds(base, 2 * ROWS), :]
        new = []
        for k in range(K):
            first = ROWS - (K - 1) + k
            taps = grad * window[first : first + ROWS]
            new.append(carry[k] + jnp.sum(taps, axis=0, keepdims=True))
        new.append(carry[K] + jnp.sum(grad, axis=0, keepdims=True))
        return tuple(new)

    sums = lax.fori_loop(0, nb, conv_block, (jnp.zeros((1, C), F32),) * (K + 1))
    halo2 = remote(dc_v.at[pl.ds(0, 8)], halo2_v, h2s, h2r, {"ctx": prv})
    halo2.start()
    for k in range(K + 1):
        oth_v[k : k + 1, :] = sums[k]
    gc_v[...] = dot(back[R:], co_v[...], 1, 0)
    for p in range(Z):
        at = nz * CB
        for i in range(other):
            j, l = divmod(p * other + i, CB)
            mf_v[p, at : at + 1, :] = oth_v[j : j + 1, lanes(l)]
            at += 1
        for i in range(coef):
            for l in range(CB):
                n = p * coef + i
                mf_v[p, at : at + 1, :] = gc_v[n : n + 1, lanes(l)]
                at += 1
    mbuf[...] = mf_v[...].astype(BF16)
    mrecv[z] = mbuf[z]
    to_ctx(lambda p: mbuf.at[p], mrecv.at[z], sm_s, sm_r)
    ring(0, gs_v, 4)
    ring(1, gp_v, 1)

    halo2.wait_recv()
    dc_v[pl.ds(T, 8), :] = jnp.where(z == Z - 1, 0.0, halo2_v[...])

    @pl.loop(0, nb)
    def _(b):
        base = pl.multiple_of(b * ROWS, ROWS)
        window = dc_v[pl.ds(base, ROWS + 8), :]
        total = jnp.zeros((ROWS, C), F32)
        for k in range(K):
            lead = K - 1 - k
            total = total + cw_v[k : k + 1, :] * window[lead : lead + ROWS]
        gin_o[pl.ds(base, ROWS), :] = total.astype(BF16)

    store(0)
    ring(0, gs_v, 5)
    ring(1, gp_v, 2)
    settle(mrecv.at[pl.ds(0, Z - 1)], sm_r)
    total = mrecv[0].astype(F32)
    for d in range(1, Z):
        total = total + mrecv[d].astype(F32)
    ag_v[z] = total[0 : ag_v.shape[1]]
    to_ctx(lambda p: ag_v.at[z], ag_v.at[z], sg_s, sg_r)
    for i in range(coef):
        for l in range(CB):
            row = nz * CB + other + i * CB + l
            gcoef_o[i : i + 1, lanes(l)] = total[row : row + 1]
    store(3)
    ring(0, gs_v, 6)
    ring(1, gp_v, 3)
    ring(0, gs_v, 7)
    ring(1, gp_v, 4)
    gstep_o[...] = ring_end(0, gs_v)
    store(4)
    ring(1, gp_v, 5)
    settle(ag_v.at[pl.ds(0, Z - 1)], sg_r)
    outs = [gcw_o.at[k : k + 1] for k in range(K)] + [gcb_o, gsb_o, gsk_o]
    for p in range(Z):
        at = 0
        for i in range(nz):
            for l in range(CB):
                n = p * nz + i
                gdl_o[n : n + 1, lanes(l)] = ag_v[p, at : at + 1, :]
                at += 1
        for i in range(other):
            j, l = divmod(p * other + i, CB)
            if j < len(outs):
                outs[j][:, lanes(l)] = ag_v[p, at : at + 1, :]
            at += 1
    for i in range(5, 10):
        store(i)
    ring(1, gp_v, 6)
    ring(1, gp_v, 7)
    gproj_o[...] = ring_end(1, gp_v)
    store(2)
    halo.wait_send()
    halo2.wait_send()
    sums_settle(1)
    for buf, sem in (
        (stot_v, ss_s), (es_v, es_s), (eo_v, ep_s), (hs_v, hs_s), (ho_v, hp_s), (mbuf, sm_s), (ag_v, sg_s),
    ):
        settle(buf.at[pl.ds(0, Z - 1)], sem)
    for i in range(10):
        pltpu.make_async_copy(outs_v[i], outs_h[i], osem.at[i]).wait()


def hand_on(*refs):
    given, held, result = refs[0:10], refs[20:30], refs[10:20]
    came, went = refs[30:]
    fetch = [pltpu.make_async_copy(a, b, came.at[i]) for i, (a, b) in enumerate(zip(given, held))]
    place = [pltpu.make_async_copy(a, b, went.at[i]) for i, (a, b) in enumerate(zip(held, result))]
    for copy in fetch:
        copy.start()
    for get, put in zip(fetch, place):
        get.wait()
        put.start()
    for copy in place:
        copy.wait()


def body(sizes, *args):
    Z, Y, T, C, R, N, K = sizes
    conv_input, gate, og, cw, cb, pw, sw, sb, dl, sk = args
    CB = C // LANE
    nz = N // Z
    rz = R // Z
    L = Z // 2
    M = max(Z - 1 - L, 1)
    coef = 2 * N // Z
    other = 8 * CB // Z
    er = nz * CB
    small = -(-(er + other + coef * CB) // ROWS) * ROWS
    back = -(-(er + other) // 8) * 8
    half = Y // 2 + 1
    vm = pltpu.VMEM
    dma = pltpu.SemaphoreType.DMA
    scratch = [
        vm((T, C), BF16), vm((T, C), BF16), vm((T, C), BF16), vm((K, C), F32), vm((1, C), F32),
        vm((R + 2 * N, C), BF16), vm((R, C), BF16), vm((1, C), F32), vm((N, C), F32), vm((1, C), F32),
        vm((ROWS, C), BF16), vm((T + ROWS, C), F32), vm((T, C), F32), vm((T, C), BF16), vm((T, C), F32),
        vm((Y + 2, ROWS, LANE), BF16), vm((half, ROWS, LANE), BF16), vm((half, ROWS, LANE), BF16),
        vm((Y // 2, 2, ROWS, LANE), BF16), vm((Y + 2, ROWS, LANE), BF16),
        vm((R, T), BF16), vm((2 * N, T), F32), vm((T, 2 * N, LANE), F32),
        *[vm((T, C), F32) for _ in range(6)],
        vm((Z, CB, LANE), F32), vm((Z, er, LANE), F32), vm((N, C), F32), vm((N, CB, LANE), F32),
        vm((T, N, C), F32), vm((T, N, C), F32),
        *[vm((Z, er, LANE), F32) for _ in range(8)], vm((N, C), F32), vm((N, C), F32),
        vm((T, C), F32), vm((T, C), F32), vm((T, C), F32), vm((T, C), BF16), vm((T, C), F32), vm((N, C), F32),
        vm((Z, rz, C), F32), vm((Z, rz, C), F32), vm((2 * N, C), F32), vm((T + 8, C), F32),
        vm((8, C), F32), vm((8, C), F32),
        vm((Z, small, LANE), F32), vm((Z, small, LANE), BF16), vm((Z, small, LANE), BF16),
        vm((Z, back, LANE), F32),
        vm((2, L, rz, C), BF16), vm((2, L, rz, C), BF16), vm((2, M, rz, C), BF16), vm((2, M, rz, C), BF16),
        dma((10,)), dma((10,)), *[dma(()) for _ in range(18)], dma((2, 4)), dma((2, 4)),
        dma((2, L)), dma((2, L)), dma((2, M)), dma((2, M)),
    ]
    shape = jax.ShapeDtypeStruct
    kinds = [
        shape((T, C), BF16), shape((T, C), BF16), shape((rz, C), F32), shape((coef, C), F32),
        shape((rz, C), F32), shape((K, C), F32), shape((1, C), F32), shape((1, C), F32),
        shape((N, C), F32), shape((1, C), F32),
    ]
    hbm = [pl.BlockSpec(memory_space=pltpu.HBM)] * 10
    outs = pl.pallas_call(
        functools.partial(kernel, sizes),
        out_shape=kinds,
        in_specs=hbm,
        out_specs=hbm,
        scratch_shapes=[vm(k.shape, k.dtype) for k in kinds] + scratch,
        compiler_params=pltpu.CompilerParams(
            collective_id=0, has_side_effects=True, vmem_limit_bytes=VMEM_BYTES
        ),
    )(conv_input, gate, og, cw, cb[None], pw, sw, sb[None], dl, sk[None])
    outs = pl.pallas_call(
        hand_on, out_shape=kinds, in_specs=hbm, out_specs=hbm,
        scratch_shapes=[vm(k.shape, k.dtype) for k in kinds] + [dma((10,)), dma((10,))],
    )(*outs)
    flat = lambda a: a.reshape(-1)
    return (*outs[:6], flat(outs[6]), flat(outs[7]), outs[8], flat(outs[9]))


def solution(mesh):
    Z, Y = mesh.shape["ctx"], mesh.shape["chan"]

    def run(conv_input, *rest):
        cw, pw, sw, dl = rest[2], rest[4], rest[5], rest[7]
        sizes = (
            Z, Y, conv_input.shape[0] // Z, conv_input.shape[1] // Y,
            sw.shape[0], dl.shape[0], cw.shape[0],
        )
        return jax.shard_map(
            functools.partial(body, sizes), mesh=mesh, in_specs=in_specs, out_specs=out_specs,
            check_vma=False,
        )(conv_input, *rest)

    both, wide, flat = P("ctx", "chan"), P(None, "chan"), P("chan")
    in_specs = (both, both, both, wide, flat, wide, wide, flat, wide, flat)
    out_specs = (both, both, both, both, both, wide, flat, flat, wide, flat)
    return run
```

```python
import functools

import jax
import jax.numpy as jnp
from jax import lax
from jax.experimental import pallas as pl
from jax.experimental.pallas import tpu as pltpu
from jax.sharding import PartitionSpec as P

LANE = 128
ROWS = 16
LOG2E = 1.4426950408889634
VMEM_BYTES = 60 * 2**20
F32 = jnp.float32
BF16 = jnp.bfloat16
MESH = pl.DeviceIdType.MESH


def group_size(count):
    return 4 if count % 4 == 0 else count


def dot(a, b, over_a, over_b):
    return lax.dot_general(
        a, b, (((over_a,), (over_b,)), ((), ())), preferred_element_type=F32
    )


def kernel(sizes, *refs):
    Z, Y, T, C, R, N, K = sizes
    CB = C // LANE
    nz = N // Z
    Q = Y // 2
    coef = 2 * N // Z
    rz = R // Z
    G = group_size(Z)
    NG = Z // G
    rb = rz // ROWS
    L = Z // 2
    M = Z - 1 - L
    nb = T // ROWS
    (
        x_h, gate_h, og_h, cw_h, cb_h, pw_h, sw_h, sb_h, dl_h, sk_h,
        gin_h, ggate_h, gproj_h, gcoef_h, gstep_h, gcw_h, gcb_h, gsb_h, gdl_h, gsk_h,
        gin_o, ggate_o, gproj_o, gcoef_o, gstep_o, gcw_o, gcb_o, gsb_o, gdl_o, gsk_o,
        x_v, gate_v, og_v, cw_v, cb_v, pw_v, sw_v, sb_v, dl_v, sk_v,
        halo_v, xe_v, slope_v, co_g, cv_v, sbuf, rbuf, gbuf, sl_v, bc_v,
        st_v, sig_v, dr_v, g_v, gg_v, sp_v, stot_v, dec_v, a2_v, a3_v, f_v, hist_v,
        es_v, er_v, eo_v, ep_v, hs_v, hr_v, ho_v, hp_v, sin_v, cin_v,
        so_v, dd_v, ab_v, pre_v, cg_v, dg_v,
        gs_v, gp_v, bp_g, gc_v, dc_v, halo2_v, oth_v, mf_v, mbuf, mrecv, ag_v,
        gp_x, gp_y, lsend, lrecv, msend, mrcv2,
        lsem, osem, hs, hr, h2s, h2r, ss_s, ss_r, es_s, es_r, ep_s, ep_r, hs_s, hs_r, hp_s, hp_r,
        sm_s, sm_r, sg_s, sg_r, send_sums, recv_sums, send_group, recv_group, send_last, recv_last, ls_s, ls_r, ms_s, ms_r,
    ) = refs
    outs_v = (gin_o, ggate_o, gproj_o, gcoef_o, gstep_o, gcw_o, gcb_o, gsb_o, gdl_o, gsk_o)
    outs_h = (gin_h, ggate_h, gproj_h, gcoef_h, gstep_h, gcw_h, gcb_h, gsb_h, gdl_h, gsk_h)
    z = lax.axis_index("ctx")
    c = lax.axis_index("chan")
    core = lax.rem(c, 2)
    chip = lax.div(c, 2)
    member = lax.rem(z, G)
    group = lax.div(z, G)
    nxt = lax.rem(z + 1, Z)
    prv = lax.rem(z + Z - 1, Z)

    def remote(src, dst, send, recv, device):
        return pltpu.make_async_remote_copy(
            src_ref=src, dst_ref=dst, send_sem=send, recv_sem=recv,
            device_id=device, device_id_type=MESH,
        )

    def settle(ref, sem):
        pltpu.make_async_copy(ref, ref, sem).wait()

    def far_first(j):
        return L + (j + 1) // 2 * (1 - 2 * (j % 2))

    def to_ctx(src_of, dst, send, recv):
        @pl.loop(0, Z - 1)
        def _(j):
            peer = lax.rem(z + far_first(j), Z)
            remote(src_of(peer), dst, send, recv, {"ctx": peer}).start()

    def lanes(l):
        return slice(LANE * l, LANE * (l + 1))

    def store(i):
        pltpu.make_async_copy(outs_v[i], outs_h[i], osem.at[i]).start()

    pairs = (
        (x_h, x_v), (cw_h, cw_v), (cb_h, cb_v), (pw_h, pw_v), (gate_h, gate_v),
        (og_h, og_v), (sw_h, sw_v), (sb_h, sb_v), (dl_h, dl_v), (sk_h, sk_v),
    )
    loads = [pltpu.make_async_copy(a, b, lsem.at[i]) for i, (a, b) in enumerate(pairs)]
    for load in loads:
        load.start()
    barrier = pltpu.get_barrier_semaphore()

    def greet(device):
        pl.semaphore_signal(barrier, inc=1, device_id=device, device_id_type=MESH)

    @pl.loop(1, Z)
    def _(k):
        greet({"ctx": lax.rem(z + far_first(Z - k - 1), Z)})

    @pl.loop(1, Y)
    def _(k):
        greet({"chan": lax.rem(c + k, Y)})

    def conv_rows(b, before):
        base = pl.multiple_of(b * ROWS, ROWS)
        rows = pl.ds(base, ROWS)
        window = jnp.concatenate([before.astype(F32), x_v[rows, :].astype(F32)], axis=0)
        xe_v[pl.ds(base, 2 * ROWS), :] = window
        pre = jnp.broadcast_to(cb_v[...], (ROWS, C))
        for k in range(K):
            lead = ROWS - (K - 1) + k
            pre = pre + cw_v[k : k + 1, :] * window[lead : lead + ROWS]
        sigma = jax.nn.sigmoid(pre)
        out = (pre * sigma).astype(BF16)
        co_g[member, rows, :] = out
        cv_v[rows, :] = out.astype(F32)
        slope_v[rows, :] = sigma * (1.0 + pre * (1.0 - sigma))

    for load in loads[:3]:
        load.wait()

    @pl.loop(1, nb)
    def _(b):
        conv_rows(b, x_v[pl.ds(pl.multiple_of((b - 1) * ROWS, ROWS), ROWS), :])

    pl.semaphore_wait(barrier, Z + Y - 2)
    halo = remote(x_v.at[pl.ds(T - ROWS, ROWS)], halo_v, hs, hr, {"ctx": nxt})
    halo.start()
    for load in loads[3:]:
        load.wait()
    a2 = -jnp.exp(dl_v[...])
    a2_v[...] = a2
    for n in range(N):
        for l in range(CB):
            a3_v[n, l : l + 1, :] = a2[n : n + 1, lanes(l)] * LOG2E
    halo.wait_recv()
    conv_rows(0, jnp.where(z == 0, 0.0, halo_v[...].astype(F32)))

    X = 4 if Q % 4 == 0 and Q > 4 else 2
    row, col = lax.div(chip, X), lax.rem(chip, X)
    offsets = sorted(
        ((dy, dx, dk) for dy in range(Q // X) for dx in range(X) for dk in range(2)),
        key=lambda o: -min(o[0], Q // X - o[0]) - min(o[1], X - o[1]),
    )
    partners = [
        (lax.rem(row + dy, Q // X) * X + lax.rem(col + dx, X)) * 2 + lax.rem(core + dk, 2)
        for dy, dx, dk in offsets
        if dy or dx or dk
    ]

    def first(d):
        return d + jnp.where(d > 0, 1, 0) + jnp.where(d > Q, 1, 0)

    def owns_two(d):
        return jnp.logical_or(d == 0, d == Q)

    mine, double = first(c), owns_two(c)
    flat_one = rbuf.at[pl.ds(0, Y - 1), pl.ds(0, 1)]
    flat_two = rbuf.at[pl.ds(0, Y - 1)]

    def either(when, yes, no):
        pl.when(when)(yes)
        pl.when(jnp.logical_not(when))(no)

    def place(p):
        at = (p % G) * NG * rb + (p // G) * rb
        return slice(at, at + rb)

    def pack(product, coefs):
        for p in range(Z):
            rows = product[rz * p : rz * (p + 1)].astype(BF16)
            sbuf[place(p)] = rows.reshape(rb, ROWS, LANE)
        sbuf[Y : Y + 2] = coefs.astype(BF16).reshape(2, ROWS, LANE)

    def unpack():
        parts = [gbuf[place(p)].reshape(rz, LANE) for p in range(Z)]
        return jnp.concatenate(parts + [gbuf[Y : Y + 2].reshape(2 * N, LANE)], axis=0)

    def scatter(which):
        send, recv = send_sums.at[which, 0], recv_sums.at[which, 0]
        for d in partners:
            at = first(d)

            def two():
                remote(sbuf.at[pl.ds(at, 2)], rbuf.at[c], send, recv, {"chan": d}).start()

            def one():
                remote(
                    sbuf.at[pl.ds(at, 1)], rbuf.at[c, pl.ds(0, 1)], send, recv, {"chan": d}
                ).start()

            either(owns_two(d), two, one)
        rbuf[c, 0] = sbuf[mine]
        rbuf[c, 1] = sbuf[jnp.minimum(mine + 1, Y + 1)]

    def spread(which):
        send, recv = send_sums.at[which, 1], recv_sums.at[which, 1]

        def part(j):
            total = rbuf[0, j].astype(F32)
            for s in range(1, Y):
                total = total + rbuf[s, j].astype(F32)
            return total.astype(BF16)

        def out(block):
            for d in partners:
                remote(block, block, send, recv, {"chan": d}).start()

        def two():
            settle(flat_two, recv_sums.at[which, 0])
            gbuf[mine] = part(0)
            gbuf[mine + 1] = part(1)
            out(gbuf.at[pl.ds(mine, 2)])
            settle(sbuf.at[pl.ds(0, Y)], send_sums.at[which, 0])

        def one():
            settle(flat_one, recv_sums.at[which, 0])
            gbuf[mine] = part(0)
            out(gbuf.at[pl.ds(mine, 1)])
            settle(sbuf.at[pl.ds(0, Y + 1)], send_sums.at[which, 0])

        either(double, two, one)

    def shared(which):
        either(
            double,
            lambda: settle(gbuf.at[pl.ds(0, Y)], recv_sums.at[which, 1]),
            lambda: settle(gbuf.at[pl.ds(0, Y + 1)], recv_sums.at[which, 1]),
        )

    def sums_settle(which):
        either(
            double,
            lambda: settle(flat_two, send_sums.at[which, 1]),
            lambda: settle(flat_one, send_sums.at[which, 1]),
        )

    def to_group(which, src_of, dst):
        for k in range(1, G):
            j = lax.rem(member + k, G)
            remote(
                src_of(j), dst, send_group.at[which], recv_group.at[which], {"ctx": group * G + j}
            ).start()

    def group_ready(which, buf):
        if G > 1:
            settle(buf.at[pl.ds(0, G - 1)], recv_group.at[which])

    def group_sent(which, buf):
        if G > 1:
            settle(buf.at[pl.ds(0, G - 1)], send_group.at[which])

    def quarter(j):
        return pl.ds(j * (NG * rb), NG * rb)

    def group_rows(left, right, total, out, back):
        parts = [left[j].reshape(NG * rz, T) for j in range(G)]
        product = dot(jnp.concatenate(parts, axis=1), right[...].reshape(G * T, C), 1, 0)
        total[...] = product.reshape(NG, rz, C)
        out[...] = product.astype(BF16).reshape(NG, rz, C)
        for k in range(1, NG):
            other = lax.rem(group + k, NG)
            remote(
                out.at[other], back.at[group], send_last, recv_last,
                {"ctx": other * G + member},
            ).start()

    def group_total(total, back):
        value = total[group]
        if NG > 1:
            settle(back.at[pl.ds(0, NG - 1)], recv_last)
            settle(back.at[pl.ds(0, NG - 1)], send_last)
        for k in range(1, NG):
            value = value + back[lax.rem(group + k, NG)].astype(F32)
        return value

    product = dot(pw_v[...], co_g[member], 1, 1)
    pack(product[0:R], product[R:])
    scatter(0)
    to_group(0, lambda j: co_g.at[member], co_g.at[member])


    @pl.loop(0, nb)
    def _(b):
        rows = pl.ds(pl.multiple_of(b * ROWS, ROWS), ROWS)
        gate = gate_v[rows, :].astype(F32)
        grad = og_v[rows, :].astype(F32)
        sigma = jax.nn.sigmoid(gate)
        g_v[rows, :] = grad * (gate * sigma)
        gg_v[rows, :] = grad * (sigma * (1.0 + gate * (1.0 - sigma)))

    spread(0)
    shared(0)

    total = unpack()
    sl_v[...] = gbuf[0:Y].reshape(R, T)
    coefs = total[R:].astype(F32)
    for t in range(T):
        bc_v[t] = jnp.broadcast_to(coefs[:, t : t + 1], (2 * N, LANE))
    sp_v[...] = dot(total[0:R], sw_v[...], 0, 0)

    def sizes_block(b, carry):
        size_sum, skip_sum = carry
        rows = pl.ds(pl.multiple_of(b * ROWS, ROWS), ROWS)
        pre = sp_v[rows, :] + sb_v[...]
        size = jnp.maximum(pre, 0.0) + jnp.log1p(jnp.exp(-jnp.abs(pre)))
        st_v[rows, :] = size
        sig_v[rows, :] = jax.nn.sigmoid(pre)
        conv = cv_v[rows, :]
        dr_v[rows, :] = size * conv
        size_sum = size_sum + jnp.sum(size, axis=0, keepdims=True)
        skip_sum = skip_sum + jnp.sum(g_v[rows, :] * conv, axis=0, keepdims=True)
        return size_sum, skip_sum

    size_sum, skip_sum = lax.fori_loop(
        0, nb, sizes_block, (jnp.zeros((1, C), F32), jnp.zeros((1, C), F32))
    )
    sums_settle(0)
    oth_v[...] = jnp.zeros_like(oth_v)
    oth_v[K + 2 : K + 3, :] = skip_sum
    for l in range(CB):
        stot_v[z, l : l + 1, :] = size_sum[:, LANE * l : LANE * (l + 1)]
    to_ctx(lambda p: stot_v.at[z], stot_v.at[z], ss_s, ss_r)

    U = 8

    def forward_local(b, h):
        a2s = a2_v[...] * LOG2E
        for i in range(U):
            t = b * U + i
            cols = bc_v[t, 0:N, :]
            size = st_v[pl.ds(t, 1), :]
            drive = dr_v[pl.ds(t, 1), :]
            f = jnp.exp2(size * a2s)
            f_v[t] = f
            h = f * h + drive * jnp.concatenate([cols] * CB, axis=1)
        return h

    end = lax.fori_loop(0, T // U, forward_local, jnp.zeros((N, C), F32))

    def rows_out(values, buf, recv_buf, send, recv):
        for n in range(N):
            p, i = divmod(n, nz)
            for l in range(CB):
                buf[p, i * CB + l : i * CB + l + 1, :] = values[n : n + 1, lanes(l)]
        recv_buf[z] = buf[z]
        to_ctx(lambda p: buf.at[p], recv_buf.at[z], send, recv)

    def rows_combine(recv_buf, out, back, order, recv, send, answer):
        settle(recv_buf.at[pl.ds(0, Z - 1)], recv)
        state = jnp.zeros((nz * CB, LANE), F32)
        for d in order:
            out[d] = state
            state = recv_buf[d] + dec_v[d] * state
        back[z] = out[z]
        to_ctx(lambda p: out.at[p], back.at[z], send, answer)

    def rows_in(back, into, recv):
        settle(back.at[pl.ds(0, Z - 1)], recv)
        for n in range(N):
            p, i = divmod(n, nz)
            for l in range(CB):
                into[n : n + 1, lanes(l)] = back[p, i * CB + l : i * CB + l + 1, :]

    rows_out(end, es_v, er_v, es_s, es_r)

    def backward_local(b, q):
        for i in range(U):
            t = T - 1 - (b * U + i)
            coefs = bc_v[t, N : 2 * N, :]
            q = f_v[t] * (jnp.concatenate([coefs] * CB, axis=1) * g_v[pl.ds(t, 1), :] + q)
        return q

    head = lax.fori_loop(0, T // U, backward_local, jnp.zeros((N, C), F32))
    rows_out(head, hs_v, hr_v, hs_s, hs_r)
    settle(stot_v.at[pl.ds(0, Z - 1)], ss_r)
    for d in range(Z):
        for i in range(nz):
            dec_v[d, i * CB : (i + 1) * CB, :] = jnp.exp2(a3_v[z * nz + i] * stot_v[d])
    rows_combine(er_v, eo_v, ep_v, range(Z), es_r, ep_s, ep_r)
    rows_combine(hr_v, ho_v, hp_v, reversed(range(Z)), hs_r, hp_s, hp_r)
    rows_in(ep_v, sin_v, ep_r)

    lane = lax.broadcasted_iota(jnp.int32, (N, LANE), 1)

    def fold(wide):
        total = wide[:, 0:LANE]
        for l in range(1, CB):
            total = total + wide[:, LANE * l : LANE * (l + 1)]
        return jnp.sum(total, axis=1, keepdims=True)

    def forward_pass(b, carry):
        h, acc = carry
        for i in range(U):
            t = b * U + i
            cols = bc_v[t]
            drive = dr_v[pl.ds(t, 1), :]
            hist_v[t] = h
            h = f_v[t] * h + drive * jnp.concatenate([cols[0:N]] * CB, axis=1)
            out = jnp.concatenate([cols[N : 2 * N]] * CB, axis=1) * h
            so_v[pl.ds(t, 1), :] = jnp.sum(out, axis=0, keepdims=True)
            acc = jnp.where(lane == t, fold(h * g_v[pl.ds(t, 1), :]), acc)
        return h, acc

    _, coef_out = lax.fori_loop(
        0, T // U, forward_pass, (sin_v[...], jnp.zeros((N, LANE), F32))
    )

    rows_in(hp_v, cin_v, hp_r)

    def backward_pass(b, carry):
        q, acc, decay = carry
        a2w = a2_v[...]
        for i in range(U):
            t = T - 1 - (b * U + i)
            cols = bc_v[t]
            g = g_v[pl.ds(t, 1), :]
            adj = jnp.concatenate([cols[N : 2 * N]] * CB, axis=1) * g + q
            q = f_v[t] * adj
            w = q * hist_v[t]
            dd_v[pl.ds(t, 1), :] = jnp.sum(a2w * w, axis=0, keepdims=True)
            ab = jnp.concatenate([cols[0:N]] * CB, axis=1) * adj
            ab_v[pl.ds(t, 1), :] = jnp.sum(ab, axis=0, keepdims=True)
            decay = decay + w * st_v[pl.ds(t, 1), :]
            acc = jnp.where(lane == t, fold(adj * dr_v[pl.ds(t, 1), :]), acc)
        return q, acc, decay

    _, coef_in, decay = lax.fori_loop(
        0, T // U, backward_pass,
        (cin_v[...], jnp.zeros((N, LANE), F32), jnp.zeros((N, C), F32)),
    )
    dg_v[...] = decay * a2_v[...]

    def pre_block(b, bias_sum):
        rows = pl.ds(pl.multiple_of(b * ROWS, ROWS), ROWS)
        pre = (dd_v[rows, :] + ab_v[rows, :] * cv_v[rows, :]) * sig_v[rows, :]
        pre_v[rows, :] = pre.astype(BF16)
        return bias_sum + jnp.sum(pre, axis=0, keepdims=True)

    oth_v[K + 1 : K + 2, :] = lax.fori_loop(0, nb, pre_block, jnp.zeros((1, C), F32))
    pack(dot(sw_v[...], pre_v[...], 1, 1), jnp.concatenate([coef_in, coef_out], axis=0))
    scatter(1)
    gs_v[...] = dot(sl_v[...], pre_v[...], 1, 0).reshape(Z, rz, C)

    def piece(p):
        return lax.rem(p, G) * NG + lax.div(p, G)

    def ring(s):
        left, right = {"ctx": prv}, {"ctx": nxt}
        if s < L:
            value = gs_v[piece(lax.rem(z + Z - L + s, Z))]
            if s:
                settle(lrecv.at[s - 1], ls_r.at[s - 1])
                value = value + lrecv[s - 1].astype(F32)
            lsend[s] = value.astype(BF16)
            remote(
                lsend.at[s], lrecv.at[s],
                ls_s.at[s], ls_r.at[s], left,
            ).start()
        if s < M:
            value = gs_v[piece(lax.rem(z + M - s, Z))]
            if s:
                settle(mrcv2.at[s - 1], ms_r.at[s - 1])
                value = value + mrcv2[s - 1].astype(F32)
            msend[s] = value.astype(BF16)
            remote(
                msend.at[s], mrcv2.at[s],
                ms_s.at[s], ms_r.at[s], right,
            ).start()

    def ring_end():
        value = gs_v[piece(z)]
        settle(lrecv.at[L - 1], ls_r.at[L - 1])
        value = value + lrecv[L - 1].astype(F32)
        if M:
            settle(mrcv2.at[M - 1], ms_r.at[M - 1])
            value = value + mrcv2[M - 1].astype(F32)
        for s in range(L):
            settle(lsend.at[s], ls_s.at[s])
        for s in range(M):
            settle(msend.at[s], ms_s.at[s])
        return value

    ring(0)

    @pl.loop(0, nb)
    def _(b):
        rows = pl.ds(pl.multiple_of(b * ROWS, ROWS), ROWS)
        skip = sk_v[...]
        ggate_o[rows, :] = (gg_v[rows, :] * (so_v[rows, :] + skip * cv_v[rows, :])).astype(BF16)
        cg_v[rows, :] = ab_v[rows, :] * st_v[rows, :] + skip * g_v[rows, :]

    store(1)

    other = 8 * CB // Z
    for p in range(Z):
        for i in range(nz):
            for l in range(CB):
                n = p * nz + i
                mf_v[p, i * CB + l : i * CB + l + 1, :] = dg_v[n : n + 1, lanes(l)]
    ring(1)
    spread(1)
    ring(2)
    shared(1)
    bp_g[member] = gbuf[quarter(member)]
    to_group(1, lambda j: gbuf.at[quarter(j)], bp_g.at[member])
    back = unpack()
    sp_v[...] = dot(back, pw_v[...], 0, 0)
    ring(3)

    def conv_block(b, carry):
        base = pl.multiple_of(b * ROWS, ROWS)
        rows = pl.ds(base, ROWS)
        grad = (cg_v[rows, :] + sp_v[rows, :]) * slope_v[rows, :]
        dc_v[rows, :] = grad
        window = xe_v[pl.ds(base, 2 * ROWS), :]
        new = []
        for k in range(K):
            first = ROWS - (K - 1) + k
            taps = grad * window[first : first + ROWS]
            new.append(carry[k] + jnp.sum(taps, axis=0, keepdims=True))
        new.append(carry[K] + jnp.sum(grad, axis=0, keepdims=True))
        return tuple(new)

    sums = lax.fori_loop(0, nb, conv_block, (jnp.zeros((1, C), F32),) * (K + 1))
    halo2 = remote(dc_v.at[pl.ds(0, 8)], halo2_v, h2s, h2r, {"ctx": prv})
    halo2.start()
    for k in range(K + 1):
        oth_v[k : k + 1, :] = sums[k]
    gc_v[...] = dot(back[R:], co_g[member], 1, 0)
    for p in range(Z):
        at = nz * CB
        for i in range(other):
            j, l = divmod(p * other + i, CB)
            mf_v[p, at : at + 1, :] = oth_v[j : j + 1, lanes(l)]
            at += 1
        for i in range(coef):
            for l in range(CB):
                n = p * coef + i
                mf_v[p, at : at + 1, :] = gc_v[n : n + 1, lanes(l)]
                at += 1
    mbuf[...] = mf_v[...].astype(BF16)
    mrecv[z] = mbuf[z]
    to_ctx(lambda p: mbuf.at[p], mrecv.at[z], sm_s, sm_r)
    ring(4)
    group_ready(0, co_g)
    group_ready(1, bp_g)
    group_rows(bp_g, co_g, gp_v, gp_x, gp_y)
    ring(5)

    halo2.wait_recv()
    dc_v[pl.ds(T, 8), :] = jnp.where(z == Z - 1, 0.0, halo2_v[...])

    @pl.loop(0, nb)
    def _(b):
        base = pl.multiple_of(b * ROWS, ROWS)
        window = dc_v[pl.ds(base, ROWS + 8), :]
        total = jnp.zeros((ROWS, C), F32)
        for k in range(K):
            lead = K - 1 - k
            total = total + cw_v[k : k + 1, :] * window[lead : lead + ROWS]
        gin_o[pl.ds(base, ROWS), :] = total.astype(BF16)

    store(0)
    ring(6)
    settle(mrecv.at[pl.ds(0, Z - 1)], sm_r)
    total = mrecv[0].astype(F32)
    for d in range(1, Z):
        total = total + mrecv[d].astype(F32)
    ag_v[z] = total[0 : ag_v.shape[1]]
    to_ctx(lambda p: ag_v.at[z], ag_v.at[z], sg_s, sg_r)
    for i in range(coef):
        for l in range(CB):
            row = nz * CB + other + i * CB + l
            gcoef_o[i : i + 1, lanes(l)] = total[row : row + 1]
    store(3)
    ring(7)
    gstep_o[...] = ring_end()
    store(4)
    settle(ag_v.at[pl.ds(0, Z - 1)], sg_r)
    outs = [gcw_o.at[k : k + 1] for k in range(K)] + [gcb_o, gsb_o, gsk_o]
    for p in range(Z):
        at = 0
        for i in range(nz):
            for l in range(CB):
                n = p * nz + i
                gdl_o[n : n + 1, lanes(l)] = ag_v[p, at : at + 1, :]
                at += 1
        for i in range(other):
            j, l = divmod(p * other + i, CB)
            if j < len(outs):
                outs[j][:, lanes(l)] = ag_v[p, at : at + 1, :]
            at += 1
    for i in range(5, 10):
        store(i)
    gproj_o[...] = group_total(gp_v, gp_y)
    store(2)
    for which, buf in ((0, co_g), (1, bp_g)):
        group_sent(which, buf)
    halo.wait_send()
    halo2.wait_send()
    sums_settle(1)
    for buf, sem in (
        (stot_v, ss_s), (es_v, es_s), (eo_v, ep_s), (hs_v, hs_s), (ho_v, hp_s), (mbuf, sm_s), (ag_v, sg_s),
    ):
        settle(buf.at[pl.ds(0, Z - 1)], sem)
    for i in range(10):
        pltpu.make_async_copy(outs_v[i], outs_h[i], osem.at[i]).wait()


def hand_on(*refs):
    given, held, result = refs[0:10], refs[20:30], refs[10:20]
    came, went = refs[30:]
    fetch = [pltpu.make_async_copy(a, b, came.at[i]) for i, (a, b) in enumerate(zip(given, held))]
    place = [pltpu.make_async_copy(a, b, went.at[i]) for i, (a, b) in enumerate(zip(held, result))]
    for copy in fetch:
        copy.start()
    for get, put in zip(fetch, place):
        get.wait()
        put.start()
    for copy in place:
        copy.wait()


def body(sizes, *args):
    Z, Y, T, C, R, N, K = sizes
    conv_input, gate, og, cw, cb, pw, sw, sb, dl, sk = args
    CB = C // LANE
    nz = N // Z
    rz = R // Z
    L = Z // 2
    M = max(Z - 1 - L, 1)
    coef = 2 * N // Z
    other = 8 * CB // Z
    er = nz * CB
    small = -(-(er + other + coef * CB) // ROWS) * ROWS
    back = -(-(er + other) // 8) * 8
    G = group_size(Z)
    NG = Z // G
    rb = rz // ROWS
    vm = pltpu.VMEM
    dma = pltpu.SemaphoreType.DMA
    scratch = [
        vm((T, C), BF16), vm((T, C), BF16), vm((T, C), BF16), vm((K, C), F32), vm((1, C), F32),
        vm((R + 2 * N, C), BF16), vm((R, C), BF16), vm((1, C), F32), vm((N, C), F32), vm((1, C), F32),
        vm((ROWS, C), BF16), vm((T + ROWS, C), F32), vm((T, C), F32), vm((G, T, C), BF16), vm((T, C), F32),
        vm((Y + 2, ROWS, LANE), BF16), vm((Y, 2, ROWS, LANE), BF16), vm((Y + 2, ROWS, LANE), BF16),
        vm((R, T), BF16), vm((T, 2 * N, LANE), F32),
        *[vm((T, C), F32) for _ in range(6)],
        vm((Z, CB, LANE), F32), vm((Z, er, LANE), F32), vm((N, C), F32), vm((N, CB, LANE), F32),
        vm((T, N, C), F32), vm((T, N, C), F32),
        *[vm((Z, er, LANE), F32) for _ in range(8)], vm((N, C), F32), vm((N, C), F32),
        vm((T, C), F32), vm((T, C), F32), vm((T, C), F32), vm((T, C), BF16), vm((T, C), F32), vm((N, C), F32),
        vm((Z, rz, C), F32), vm((NG, rz, C), F32), vm((G, NG * rb, ROWS, T), BF16), vm((2 * N, C), F32),
        vm((T + 8, C), F32),
        vm((8, C), F32), vm((8, C), F32),
        vm((Z, small, LANE), F32), vm((Z, small, LANE), BF16), vm((Z, small, LANE), BF16),
        vm((Z, back, LANE), F32),
        vm((NG, rz, C), BF16), vm((NG, rz, C), BF16),
        vm((L, rz, C), BF16), vm((L, rz, C), BF16), vm((M, rz, C), BF16), vm((M, rz, C), BF16),
        dma((10,)), dma((10,)), *[dma(()) for _ in range(18)], dma((2, 2)), dma((2, 2)),
        dma((2,)), dma((2,)), dma(()), dma(()), dma((L,)), dma((L,)), dma((M,)), dma((M,)),
    ]
    shape = jax.ShapeDtypeStruct
    kinds = [
        shape((T, C), BF16), shape((T, C), BF16), shape((rz, C), F32), shape((coef, C), F32),
        shape((rz, C), F32), shape((K, C), F32), shape((1, C), F32), shape((1, C), F32),
        shape((N, C), F32), shape((1, C), F32),
    ]
    hbm = [pl.BlockSpec(memory_space=pltpu.HBM)] * 10
    outs = pl.pallas_call(
        functools.partial(kernel, sizes),
        out_shape=kinds,
        in_specs=hbm,
        out_specs=hbm,
        scratch_shapes=[vm(k.shape, k.dtype) for k in kinds] + scratch,
        compiler_params=pltpu.CompilerParams(
            collective_id=0, has_side_effects=True, vmem_limit_bytes=VMEM_BYTES
        ),
    )(conv_input, gate, og, cw, cb[None], pw, sw, sb[None], dl, sk[None])
    outs = pl.pallas_call(
        hand_on, out_shape=kinds, in_specs=hbm, out_specs=hbm,
        scratch_shapes=[vm(k.shape, k.dtype) for k in kinds] + [dma((10,)), dma((10,))],
    )(*outs)
    flat = lambda a: a.reshape(-1)
    return (*outs[:6], flat(outs[6]), flat(outs[7]), outs[8], flat(outs[9]))


def solution(mesh):
    Z, Y = mesh.shape["ctx"], mesh.shape["chan"]

    def run(conv_input, *rest):
        cw, pw, sw, dl = rest[2], rest[4], rest[5], rest[7]
        sizes = (
            Z, Y, conv_input.shape[0] // Z, conv_input.shape[1] // Y,
            sw.shape[0], dl.shape[0], cw.shape[0],
        )
        return jax.shard_map(
            functools.partial(body, sizes), mesh=mesh, in_specs=in_specs, out_specs=out_specs,
            check_vma=False,
        )(conv_input, *rest)

    both, wide, flat = P("ctx", "chan"), P(None, "chan"), P("chan")
    in_specs = (both, both, both, wide, flat, wide, wide, flat, wide, flat)
    out_specs = (both, both, both, both, both, wide, flat, flat, wide, flat)
    return run
```

```python
import functools

import jax
import jax.numpy as jnp
from jax import lax
from jax.experimental import pallas as pl
from jax.experimental.pallas import tpu as pltpu
from jax.sharding import PartitionSpec as P

LANE = 128
ROWS = 16
LOG2E = 1.4426950408889634
VMEM_BYTES = 60 * 2**20
F32 = jnp.float32
BF16 = jnp.bfloat16
MESH = pl.DeviceIdType.MESH


def group_size(count):
    return 4 if count % 4 == 0 else count


def dot(a, b, over_a, over_b):
    return lax.dot_general(
        a, b, (((over_a,), (over_b,)), ((), ())), preferred_element_type=F32
    )


def kernel(sizes, *refs):
    Z, Y, T, C, R, N, K = sizes
    CB = C // LANE
    nz = N // Z
    Q = Y // 2
    coef = 2 * N // Z
    rz = R // Z
    G = group_size(Z)
    NG = Z // G
    rb = rz // ROWS
    L = Z // 2
    M = Z - 1 - L
    nb = T // ROWS
    (
        x_h, gate_h, og_h, cw_h, cb_h, pw_h, sw_h, sb_h, dl_h, sk_h,
        gin_h, ggate_h, gproj_h, gcoef_h, gstep_h, gcw_h, gcb_h, gsb_h, gdl_h, gsk_h,
        gin_o, ggate_o, gproj_o, gcoef_o, gstep_o, gcw_o, gcb_o, gsb_o, gdl_o, gsk_o,
        x_v, gate_v, og_v, cw_v, cb_v, pw_v, sw_v, sb_v, dl_v, sk_v,
        halo_v, xe_v, slope_v, co_g, cv_v, sbuf, rbuf, gbuf, sl_v, bc_v,
        st_v, sig_v, dr_v, g_v, gg_v, sp_v, dec_v, a2_v, a3_v, f_v, hist_v,
        es_v, er_v, eo_v, ep_v, hs_v, hr_v, ho_v, hp_v, sin_v, cin_v,
        so_v, dd_v, ab_v, pre_v, cg_v, dg_v,
        gs_v, gp_v, bp_g, gc_v, dc_v, halo2_v, oth_v, few_v, kf_v, kr_v, ka_v, mf_v, mbuf, mrecv, ag_v,
        gp_x, gp_y, lsend, lrecv, msend, mrcv2,
        lsem, osem, hs, hr, h2s, h2r, kk_s, kk_r, ka_s, ka_r, es_s, es_r, ep_s, ep_r, hs_s, hs_r, hp_s, hp_r,
        sm_s, sm_r, sg_s, sg_r, send_sums, recv_sums, send_group, recv_group, send_last, recv_last, ls_s, ls_r, ms_s, ms_r,
    ) = refs
    outs_v = (gin_o, ggate_o, gproj_o, gcoef_o, gstep_o, gcw_o, gcb_o, gsb_o, gdl_o, gsk_o)
    outs_h = (gin_h, ggate_h, gproj_h, gcoef_h, gstep_h, gcw_h, gcb_h, gsb_h, gdl_h, gsk_h)
    z = lax.axis_index("ctx")
    c = lax.axis_index("chan")
    core = lax.rem(c, 2)
    chip = lax.div(c, 2)
    member = lax.rem(z, G)
    group = lax.div(z, G)
    nxt = lax.rem(z + 1, Z)
    prv = lax.rem(z + Z - 1, Z)

    def remote(src, dst, send, recv, device):
        return pltpu.make_async_remote_copy(
            src_ref=src, dst_ref=dst, send_sem=send, recv_sem=recv,
            device_id=device, device_id_type=MESH,
        )

    def settle(ref, sem):
        pltpu.make_async_copy(ref, ref, sem).wait()

    def far_first(j):
        return L + (j + 1) // 2 * (1 - 2 * (j % 2))

    def to_ctx(src_of, dst, send, recv):
        @pl.loop(0, Z - 1)
        def _(j):
            peer = lax.rem(z + far_first(j), Z)
            remote(src_of(peer), dst, send, recv, {"ctx": peer}).start()

    def lanes(l):
        return slice(LANE * l, LANE * (l + 1))

    def store(i):
        pltpu.make_async_copy(outs_v[i], outs_h[i], osem.at[i]).start()

    pairs = (
        (x_h, x_v), (cw_h, cw_v), (cb_h, cb_v), (pw_h, pw_v), (gate_h, gate_v),
        (og_h, og_v), (sw_h, sw_v), (sb_h, sb_v), (dl_h, dl_v), (sk_h, sk_v),
    )
    loads = [pltpu.make_async_copy(a, b, lsem.at[i]) for i, (a, b) in enumerate(pairs)]
    for load in loads:
        load.start()
    barrier = pltpu.get_barrier_semaphore()

    def greet(device):
        pl.semaphore_signal(barrier, inc=1, device_id=device, device_id_type=MESH)

    @pl.loop(1, Z)
    def _(k):
        greet({"ctx": lax.rem(z + far_first(Z - k - 1), Z)})

    @pl.loop(1, Y)
    def _(k):
        greet({"chan": lax.rem(c + k, Y)})

    def conv_rows(b, before):
        base = pl.multiple_of(b * ROWS, ROWS)
        rows = pl.ds(base, ROWS)
        window = jnp.concatenate([before.astype(F32), x_v[rows, :].astype(F32)], axis=0)
        xe_v[pl.ds(base, 2 * ROWS), :] = window
        pre = jnp.broadcast_to(cb_v[...], (ROWS, C))
        for k in range(K):
            lead = ROWS - (K - 1) + k
            pre = pre + cw_v[k : k + 1, :] * window[lead : lead + ROWS]
        sigma = jax.nn.sigmoid(pre)
        out = (pre * sigma).astype(BF16)
        co_g[member, rows, :] = out
        cv_v[rows, :] = out.astype(F32)
        slope_v[rows, :] = sigma * (1.0 + pre * (1.0 - sigma))

    for load in loads[:3]:
        load.wait()

    @pl.loop(1, nb)
    def _(b):
        conv_rows(b, x_v[pl.ds(pl.multiple_of((b - 1) * ROWS, ROWS), ROWS), :])

    pl.semaphore_wait(barrier, Z + Y - 2)
    halo = remote(x_v.at[pl.ds(T - ROWS, ROWS)], halo_v, hs, hr, {"ctx": nxt})
    halo.start()
    for load in loads[3:]:
        load.wait()
    a2 = -jnp.exp(dl_v[...])
    a2_v[...] = a2
    for n in range(N):
        for l in range(CB):
            a3_v[n, l : l + 1, :] = a2[n : n + 1, lanes(l)] * LOG2E
    halo.wait_recv()
    conv_rows(0, jnp.where(z == 0, 0.0, halo_v[...].astype(F32)))

    X = 4 if Q % 4 == 0 and Q > 4 else 2
    row, col = lax.div(chip, X), lax.rem(chip, X)
    offsets = sorted(
        ((dy, dx, dk) for dy in range(Q // X) for dx in range(X) for dk in range(2)),
        key=lambda o: -min(o[0], Q // X - o[0]) - min(o[1], X - o[1]),
    )
    partners = [
        (lax.rem(row + dy, Q // X) * X + lax.rem(col + dx, X)) * 2 + lax.rem(core + dk, 2)
        for dy, dx, dk in offsets
        if dy or dx or dk
    ]

    def first(d):
        return d + jnp.where(d > 0, 1, 0) + jnp.where(d > Q, 1, 0)

    def owns_two(d):
        return jnp.logical_or(d == 0, d == Q)

    mine, double = first(c), owns_two(c)
    flat_one = rbuf.at[pl.ds(0, Y - 1), pl.ds(0, 1)]
    flat_two = rbuf.at[pl.ds(0, Y - 1)]

    def either(when, yes, no):
        pl.when(when)(yes)
        pl.when(jnp.logical_not(when))(no)

    def place(p):
        at = (p % G) * NG * rb + (p // G) * rb
        return slice(at, at + rb)

    def pack(product, coefs):
        for p in range(Z):
            rows = product[rz * p : rz * (p + 1)].astype(BF16)
            sbuf[place(p)] = rows.reshape(rb, ROWS, LANE)
        sbuf[Y : Y + 2] = coefs.astype(BF16).reshape(2, ROWS, LANE)

    def unpack():
        parts = [gbuf[place(p)].reshape(rz, LANE) for p in range(Z)]
        return jnp.concatenate(parts + [gbuf[Y : Y + 2].reshape(2 * N, LANE)], axis=0)

    def scatter(which):
        send, recv = send_sums.at[which, 0], recv_sums.at[which, 0]
        for d in partners:
            at = first(d)

            def two():
                remote(sbuf.at[pl.ds(at, 2)], rbuf.at[c], send, recv, {"chan": d}).start()

            def one():
                remote(
                    sbuf.at[pl.ds(at, 1)], rbuf.at[c, pl.ds(0, 1)], send, recv, {"chan": d}
                ).start()

            either(owns_two(d), two, one)
        rbuf[c, 0] = sbuf[mine]
        rbuf[c, 1] = sbuf[jnp.minimum(mine + 1, Y + 1)]

    def spread(which):
        send, recv = send_sums.at[which, 1], recv_sums.at[which, 1]

        def part(j):
            total = rbuf[0, j].astype(F32)
            for s in range(1, Y):
                total = total + rbuf[s, j].astype(F32)
            return total.astype(BF16)

        def out(block):
            for d in partners:
                remote(block, block, send, recv, {"chan": d}).start()

        def two():
            settle(flat_two, recv_sums.at[which, 0])
            gbuf[mine] = part(0)
            gbuf[mine + 1] = part(1)
            out(gbuf.at[pl.ds(mine, 2)])
            settle(sbuf.at[pl.ds(0, Y)], send_sums.at[which, 0])

        def one():
            settle(flat_one, recv_sums.at[which, 0])
            gbuf[mine] = part(0)
            out(gbuf.at[pl.ds(mine, 1)])
            settle(sbuf.at[pl.ds(0, Y + 1)], send_sums.at[which, 0])

        either(double, two, one)

    def shared(which):
        either(
            double,
            lambda: settle(gbuf.at[pl.ds(0, Y)], recv_sums.at[which, 1]),
            lambda: settle(gbuf.at[pl.ds(0, Y + 1)], recv_sums.at[which, 1]),
        )

    def sums_settle(which):
        either(
            double,
            lambda: settle(flat_two, send_sums.at[which, 1]),
            lambda: settle(flat_one, send_sums.at[which, 1]),
        )

    def to_group(which, src_of, dst):
        for k in range(1, G):
            j = lax.rem(member + k, G)
            remote(
                src_of(j), dst, send_group.at[which], recv_group.at[which], {"ctx": group * G + j}
            ).start()

    def group_ready(which, buf):
        if G > 1:
            settle(buf.at[pl.ds(0, G - 1)], recv_group.at[which])

    def group_sent(which, buf):
        if G > 1:
            settle(buf.at[pl.ds(0, G - 1)], send_group.at[which])

    def quarter(j):
        return pl.ds(j * (NG * rb), NG * rb)

    def group_rows(left, right, total, out, back):
        parts = [left[j].reshape(NG * rz, T) for j in range(G)]
        product = dot(jnp.concatenate(parts, axis=1), right[...].reshape(G * T, C), 1, 0)
        total[...] = product.reshape(NG, rz, C)
        out[...] = product.astype(BF16).reshape(NG, rz, C)
        for k in range(1, NG):
            other = lax.rem(group + k, NG)
            remote(
                out.at[other], back.at[group], send_last, recv_last,
                {"ctx": other * G + member},
            ).start()

    def group_total(total, back):
        value = total[group]
        if NG > 1:
            settle(back.at[pl.ds(0, NG - 1)], recv_last)
            settle(back.at[pl.ds(0, NG - 1)], send_last)
        for k in range(1, NG):
            value = value + back[lax.rem(group + k, NG)].astype(F32)
        return value

    product = dot(pw_v[...], co_g[member], 1, 1)
    pack(product[0:R], product[R:])
    scatter(0)
    to_group(0, lambda j: co_g.at[member], co_g.at[member])


    @pl.loop(0, nb)
    def _(b):
        rows = pl.ds(pl.multiple_of(b * ROWS, ROWS), ROWS)
        gate = gate_v[rows, :].astype(F32)
        grad = og_v[rows, :].astype(F32)
        sigma = jax.nn.sigmoid(gate)
        g_v[rows, :] = grad * (gate * sigma)
        gg_v[rows, :] = grad * (sigma * (1.0 + gate * (1.0 - sigma)))

    spread(0)
    shared(0)

    total = unpack()
    sl_v[...] = gbuf[0:Y].reshape(R, T)
    coefs = total[R:].astype(F32)
    for t in range(T):
        bc_v[t] = jnp.broadcast_to(coefs[:, t : t + 1], (2 * N, LANE))
    sp_v[...] = dot(total[0:R], sw_v[...], 0, 0)

    def sizes_block(b, carry):
        size_sum, skip_sum = carry
        rows = pl.ds(pl.multiple_of(b * ROWS, ROWS), ROWS)
        pre = sp_v[rows, :] + sb_v[...]
        size = jnp.maximum(pre, 0.0) + jnp.log1p(jnp.exp(-jnp.abs(pre)))
        st_v[rows, :] = size
        sig_v[rows, :] = jax.nn.sigmoid(pre)
        conv = cv_v[rows, :]
        dr_v[rows, :] = size * conv
        size_sum = size_sum + jnp.sum(size, axis=0, keepdims=True)
        skip_sum = skip_sum + jnp.sum(g_v[rows, :] * conv, axis=0, keepdims=True)
        return size_sum, skip_sum

    size_sum, skip_sum = lax.fori_loop(
        0, nb, sizes_block, (jnp.zeros((1, C), F32), jnp.zeros((1, C), F32))
    )
    sums_settle(0)
    oth_v[...] = jnp.zeros_like(oth_v)
    few_v[...] = jnp.zeros_like(few_v)
    few_v[1:2, :] = skip_sum
    U = 32

    def forward_local(b, h):
        a2s = a2_v[...] * LOG2E
        for i in range(U):
            t = b * U + i
            cols = bc_v[t, 0:N, :]
            size = st_v[pl.ds(t, 1), :]
            drive = dr_v[pl.ds(t, 1), :]
            f = jnp.exp2(size * a2s)
            f_v[t] = f
            h = f * h + drive * jnp.concatenate([cols] * CB, axis=1)
        return h

    end = lax.fori_loop(0, T // U, forward_local, jnp.zeros((N, C), F32))

    def rows_out(values, buf, recv_buf, send, recv, extra=None):
        for n in range(N):
            p, i = divmod(n, nz)
            for l in range(CB):
                buf[p, i * CB + l : i * CB + l + 1, :] = values[n : n + 1, lanes(l)]
        if extra is not None:
            for l in range(CB):
                row = jnp.broadcast_to(extra[:, lanes(l)].reshape(1, 1, LANE), (Z, 1, LANE))
                buf[:, nz * CB + l : nz * CB + l + 1, :] = row
        recv_buf[z] = buf[z]
        to_ctx(lambda p: buf.at[p], recv_buf.at[z], send, recv)

    def rows_combine(recv_buf, out, back, order, recv, send, answer):
        if recv is not None:
            settle(recv_buf.at[pl.ds(0, Z - 1)], recv)
        state = jnp.zeros((nz * CB, LANE), F32)
        for d in order:
            out[d] = state
            state = recv_buf[d, 0 : nz * CB, :] + dec_v[d] * state
        back[z] = out[z]
        to_ctx(lambda p: out.at[p], back.at[z], send, answer)

    def rows_in(back, into, recv):
        settle(back.at[pl.ds(0, Z - 1)], recv)
        for n in range(N):
            p, i = divmod(n, nz)
            for l in range(CB):
                into[n : n + 1, lanes(l)] = back[p, i * CB + l : i * CB + l + 1, :]

    rows_out(end, es_v, er_v, es_s, es_r, size_sum)

    def backward_local(b, q):
        for i in range(U):
            t = T - 1 - (b * U + i)
            coefs = bc_v[t, N : 2 * N, :]
            q = f_v[t] * (jnp.concatenate([coefs] * CB, axis=1) * g_v[pl.ds(t, 1), :] + q)
        return q

    head = lax.fori_loop(0, T // U, backward_local, jnp.zeros((N, C), F32))
    rows_out(head, hs_v, hr_v, hs_s, hs_r)
    settle(er_v.at[pl.ds(0, Z - 1)], es_r)
    for d in range(Z):
        for i in range(nz):
            total_size = er_v[d, nz * CB : (nz + 1) * CB, :]
            dec_v[d, i * CB : (i + 1) * CB, :] = jnp.exp2(a3_v[z * nz + i] * total_size)
    rows_combine(er_v, eo_v, ep_v, range(Z), None, ep_s, ep_r)
    rows_combine(hr_v, ho_v, hp_v, reversed(range(Z)), hs_r, hp_s, hp_r)
    rows_in(ep_v, sin_v, ep_r)

    lane = lax.broadcasted_iota(jnp.int32, (N, LANE), 1)

    def fold(wide):
        total = wide[:, 0:LANE]
        for l in range(1, CB):
            total = total + wide[:, LANE * l : LANE * (l + 1)]
        return jnp.sum(total, axis=1, keepdims=True)

    def forward_pass(b, carry):
        h, acc = carry
        for i in range(U):
            t = b * U + i
            cols = bc_v[t]
            drive = dr_v[pl.ds(t, 1), :]
            hist_v[t] = h
            h = f_v[t] * h + drive * jnp.concatenate([cols[0:N]] * CB, axis=1)
            out = jnp.concatenate([cols[N : 2 * N]] * CB, axis=1) * h
            so_v[pl.ds(t, 1), :] = jnp.sum(out, axis=0, keepdims=True)
            acc = jnp.where(lane == t, fold(h * g_v[pl.ds(t, 1), :]), acc)
        return h, acc

    _, coef_out = lax.fori_loop(
        0, T // U, forward_pass, (sin_v[...], jnp.zeros((N, LANE), F32))
    )

    rows_in(hp_v, cin_v, hp_r)

    def backward_pass(b, carry):
        q, acc, decay = carry
        a2w = a2_v[...]
        for i in range(U):
            t = T - 1 - (b * U + i)
            cols = bc_v[t]
            g = g_v[pl.ds(t, 1), :]
            adj = jnp.concatenate([cols[N : 2 * N]] * CB, axis=1) * g + q
            q = f_v[t] * adj
            w = q * hist_v[t]
            dd_v[pl.ds(t, 1), :] = jnp.sum(a2w * w, axis=0, keepdims=True)
            ab = jnp.concatenate([cols[0:N]] * CB, axis=1) * adj
            ab_v[pl.ds(t, 1), :] = jnp.sum(ab, axis=0, keepdims=True)
            decay = decay + w * st_v[pl.ds(t, 1), :]
            acc = jnp.where(lane == t, fold(adj * dr_v[pl.ds(t, 1), :]), acc)
        return q, acc, decay

    _, coef_in, decay = lax.fori_loop(
        0, T // U, backward_pass,
        (cin_v[...], jnp.zeros((N, LANE), F32), jnp.zeros((N, C), F32)),
    )
    dg_v[...] = decay * a2_v[...]

    def pre_block(b, bias_sum):
        rows = pl.ds(pl.multiple_of(b * ROWS, ROWS), ROWS)
        pre = (dd_v[rows, :] + ab_v[rows, :] * cv_v[rows, :]) * sig_v[rows, :]
        pre_v[rows, :] = pre.astype(BF16)
        return bias_sum + jnp.sum(pre, axis=0, keepdims=True)

    few_v[0:1, :] = lax.fori_loop(0, nb, pre_block, jnp.zeros((1, C), F32))
    pack(dot(sw_v[...], pre_v[...], 1, 1), jnp.concatenate([coef_in, coef_out], axis=0))
    scatter(1)
    gs_v[...] = dot(sl_v[...], pre_v[...], 1, 0).reshape(Z, rz, C)

    def piece(p):
        return lax.rem(p, G) * NG + lax.div(p, G)

    def ring(s):
        left, right = {"ctx": prv}, {"ctx": nxt}
        if s < L:
            value = gs_v[piece(lax.rem(z + Z - L + s, Z))]
            if s:
                settle(lrecv.at[s - 1], ls_r.at[s - 1])
                value = value + lrecv[s - 1].astype(F32)
            lsend[s] = value.astype(BF16)
            remote(
                lsend.at[s], lrecv.at[s],
                ls_s.at[s], ls_r.at[s], left,
            ).start()
        if s < M:
            value = gs_v[piece(lax.rem(z + M - s, Z))]
            if s:
                settle(mrcv2.at[s - 1], ms_r.at[s - 1])
                value = value + mrcv2[s - 1].astype(F32)
            msend[s] = value.astype(BF16)
            remote(
                msend.at[s], mrcv2.at[s],
                ms_s.at[s], ms_r.at[s], right,
            ).start()

    def ring_end():
        value = gs_v[piece(z)]
        settle(lrecv.at[L - 1], ls_r.at[L - 1])
        value = value + lrecv[L - 1].astype(F32)
        if M:
            settle(mrcv2.at[M - 1], ms_r.at[M - 1])
            value = value + mrcv2[M - 1].astype(F32)
        for s in range(L):
            settle(lsend.at[s], ls_s.at[s])
        for s in range(M):
            settle(msend.at[s], ms_s.at[s])
        return value

    ring(0)

    @pl.loop(0, nb)
    def _(b):
        rows = pl.ds(pl.multiple_of(b * ROWS, ROWS), ROWS)
        skip = sk_v[...]
        ggate_o[rows, :] = (gg_v[rows, :] * (so_v[rows, :] + skip * cv_v[rows, :])).astype(BF16)
        cg_v[rows, :] = ab_v[rows, :] * st_v[rows, :] + skip * g_v[rows, :]

    store(1)

    def rows_of(p, source, count):
        for i in range(count):
            n, l = divmod(p * count + i, CB)
            yield i, source, n, l

    def sum_rows(buf, recv_buf, back_buf, recv, send, answer, rows):
        settle(recv_buf.at[pl.ds(0, Z - 1)], recv)
        total = recv_buf[0].astype(F32)
        for d in range(1, Z):
            total = total + recv_buf[d].astype(F32)
        back_buf[z] = total[0:rows]
        to_ctx(lambda p: back_buf.at[z], back_buf.at[z], send, answer)
        return total

    few = 4 * CB // Z
    for p in range(Z):
        for i, ref, n, l in rows_of(p, dg_v, nz * CB):
            kf_v[p, i : i + 1, :] = ref[n : n + 1, lanes(l)]
        for i, ref, n, l in rows_of(p, few_v, few):
            kf_v[p, nz * CB + i : nz * CB + i + 1, :] = ref[n : n + 1, lanes(l)]
    kr_v[z] = kf_v[z]
    to_ctx(lambda p: kf_v.at[p], kr_v.at[z], kk_s, kk_r)
    ring(1)
    spread(1)
    ring(2)
    sum_rows(kf_v, kr_v, ka_v, kk_r, ka_s, ka_r, nz * CB + few)
    shared(1)
    ring(3)
    bp_g[member] = gbuf[quarter(member)]
    to_group(1, lambda j: gbuf.at[quarter(j)], bp_g.at[member])
    back = unpack()
    sp_v[...] = dot(back, pw_v[...], 0, 0)

    def conv_block(b, carry):
        base = pl.multiple_of(b * ROWS, ROWS)
        rows = pl.ds(base, ROWS)
        grad = (cg_v[rows, :] + sp_v[rows, :]) * slope_v[rows, :]
        dc_v[rows, :] = grad
        window = xe_v[pl.ds(base, 2 * ROWS), :]
        new = []
        for k in range(K):
            first = ROWS - (K - 1) + k
            taps = grad * window[first : first + ROWS]
            new.append(carry[k] + jnp.sum(taps, axis=0, keepdims=True))
        new.append(carry[K] + jnp.sum(grad, axis=0, keepdims=True))
        return tuple(new)

    sums = lax.fori_loop(0, nb, conv_block, (jnp.zeros((1, C), F32),) * (K + 1))
    halo2 = remote(dc_v.at[pl.ds(0, 8)], halo2_v, h2s, h2r, {"ctx": prv})
    halo2.start()
    for k in range(K + 1):
        oth_v[k : k + 1, :] = sums[k]
    gc_v[...] = dot(back[R:], co_g[member], 1, 0)
    other = 8 * CB // Z
    for p in range(Z):
        for i, ref, n, l in rows_of(p, oth_v, other):
            mf_v[p, i : i + 1, :] = ref[n : n + 1, lanes(l)]
        for i, ref, n, l in rows_of(p, gc_v, coef * CB):
            mf_v[p, other + i : other + i + 1, :] = ref[n : n + 1, lanes(l)]
    mbuf[...] = mf_v[...].astype(BF16)
    mrecv[z] = mbuf[z]
    to_ctx(lambda p: mbuf.at[p], mrecv.at[z], sm_s, sm_r)
    ring(4)
    group_ready(0, co_g)
    group_ready(1, bp_g)
    group_rows(bp_g, co_g, gp_v, gp_x, gp_y)
    ring(5)

    halo2.wait_recv()
    dc_v[pl.ds(T, 8), :] = jnp.where(z == Z - 1, 0.0, halo2_v[...])

    @pl.loop(0, nb)
    def _(b):
        base = pl.multiple_of(b * ROWS, ROWS)
        window = dc_v[pl.ds(base, ROWS + 8), :]
        total = jnp.zeros((ROWS, C), F32)
        for k in range(K):
            lead = K - 1 - k
            total = total + cw_v[k : k + 1, :] * window[lead : lead + ROWS]
        gin_o[pl.ds(base, ROWS), :] = total.astype(BF16)

    store(0)
    total = sum_rows(mbuf, mrecv, ag_v, sm_r, sg_s, sg_r, other)
    for i in range(coef):
        for l in range(CB):
            at = other + i * CB + l
            gcoef_o[i : i + 1, lanes(l)] = total[at : at + 1]
    store(3)
    ring(6)
    ring(7)
    settle(ka_v.at[pl.ds(0, Z - 1)], ka_r)
    for p in range(Z):
        for i, ref, n, l in rows_of(p, gdl_o, nz * CB):
            ref[n : n + 1, lanes(l)] = ka_v[p, i : i + 1, :]
        for i, _, n, l in rows_of(p, None, few):
            if n < 2:
                (gsb_o, gsk_o)[n][:, lanes(l)] = ka_v[p, nz * CB + i : nz * CB + i + 1, :]
    for i in (7, 8, 9):
        store(i)
    gstep_o[...] = ring_end()
    store(4)
    settle(ag_v.at[pl.ds(0, Z - 1)], sg_r)
    for p in range(Z):
        for i, _, n, l in rows_of(p, None, other):
            if n < K:
                gcw_o[n : n + 1, lanes(l)] = ag_v[p, i : i + 1, :]
            elif n == K:
                gcb_o[:, lanes(l)] = ag_v[p, i : i + 1, :]
    for i in (5, 6):
        store(i)
    gproj_o[...] = group_total(gp_v, gp_y)
    store(2)
    for which, buf in ((0, co_g), (1, bp_g)):
        group_sent(which, buf)
    halo.wait_send()
    halo2.wait_send()
    sums_settle(1)
    for buf, sem in (
        (es_v, es_s), (eo_v, ep_s), (hs_v, hs_s), (ho_v, hp_s), (mbuf, sm_s), (ag_v, sg_s), (kf_v, kk_s), (ka_v, ka_s),
    ):
        settle(buf.at[pl.ds(0, Z - 1)], sem)
    for i in range(10):
        pltpu.make_async_copy(outs_v[i], outs_h[i], osem.at[i]).wait()


def hand_on(*refs):
    given, held, result = refs[0:10], refs[20:30], refs[10:20]
    came, went = refs[30:]
    fetch = [pltpu.make_async_copy(a, b, came.at[i]) for i, (a, b) in enumerate(zip(given, held))]
    place = [pltpu.make_async_copy(a, b, went.at[i]) for i, (a, b) in enumerate(zip(held, result))]
    for copy in fetch:
        copy.start()
    for get, put in zip(fetch, place):
        get.wait()
        put.start()
    for copy in place:
        copy.wait()


def body(sizes, *args):
    Z, Y, T, C, R, N, K = sizes
    conv_input, gate, og, cw, cb, pw, sw, sb, dl, sk = args
    CB = C // LANE
    nz = N // Z
    rz = R // Z
    L = Z // 2
    M = max(Z - 1 - L, 1)
    coef = 2 * N // Z
    other = 8 * CB // Z
    er = nz * CB
    few = 4 * CB // Z
    kept = -(-(er + few) // 8) * 8
    small = -(-(other + coef * CB) // ROWS) * ROWS
    G = group_size(Z)
    NG = Z // G
    rb = rz // ROWS
    vm = pltpu.VMEM
    dma = pltpu.SemaphoreType.DMA
    scratch = [
        vm((T, C), BF16), vm((T, C), BF16), vm((T, C), BF16), vm((K, C), F32), vm((1, C), F32),
        vm((R + 2 * N, C), BF16), vm((R, C), BF16), vm((1, C), F32), vm((N, C), F32), vm((1, C), F32),
        vm((ROWS, C), BF16), vm((T + ROWS, C), F32), vm((T, C), F32), vm((G, T, C), BF16), vm((T, C), F32),
        vm((Y + 2, ROWS, LANE), BF16), vm((Y, 2, ROWS, LANE), BF16), vm((Y + 2, ROWS, LANE), BF16),
        vm((R, T), BF16), vm((T, 2 * N, LANE), F32),
        *[vm((T, C), F32) for _ in range(6)],
        vm((Z, er, LANE), F32), vm((N, C), F32), vm((N, CB, LANE), F32),
        vm((T, N, C), F32), vm((T, N, C), F32),
        *[vm((Z, er + CB, LANE), F32) for _ in range(2)], *[vm((Z, er, LANE), F32) for _ in range(6)],
        vm((N, C), F32), vm((N, C), F32),
        vm((T, C), F32), vm((T, C), F32), vm((T, C), F32), vm((T, C), BF16), vm((T, C), F32), vm((N, C), F32),
        vm((Z, rz, C), F32), vm((NG, rz, C), F32), vm((G, NG * rb, ROWS, T), BF16), vm((2 * N, C), F32),
        vm((T + 8, C), F32),
        vm((8, C), F32), vm((8, C), F32), vm((4, C), F32),
        vm((Z, kept, LANE), F32), vm((Z, kept, LANE), F32), vm((Z, er + few, LANE), F32),
        vm((Z, small, LANE), F32), vm((Z, small, LANE), BF16), vm((Z, small, LANE), BF16),
        vm((Z, other, LANE), F32),
        vm((NG, rz, C), BF16), vm((NG, rz, C), BF16),
        vm((L, rz, C), BF16), vm((L, rz, C), BF16), vm((M, rz, C), BF16), vm((M, rz, C), BF16),
        dma((10,)), dma((10,)), *[dma(()) for _ in range(20)], dma((2, 2)), dma((2, 2)),
        dma((2,)), dma((2,)), dma(()), dma(()), dma((L,)), dma((L,)), dma((M,)), dma((M,)),
    ]
    shape = jax.ShapeDtypeStruct
    kinds = [
        shape((T, C), BF16), shape((T, C), BF16), shape((rz, C), F32), shape((coef, C), F32),
        shape((rz, C), F32), shape((K, C), F32), shape((1, C), F32), shape((1, C), F32),
        shape((N, C), F32), shape((1, C), F32),
    ]
    hbm = [pl.BlockSpec(memory_space=pltpu.HBM)] * 10
    outs = pl.pallas_call(
        functools.partial(kernel, sizes),
        out_shape=kinds,
        in_specs=hbm,
        out_specs=hbm,
        scratch_shapes=[vm(k.shape, k.dtype) for k in kinds] + scratch,
        compiler_params=pltpu.CompilerParams(
            collective_id=0, has_side_effects=True, vmem_limit_bytes=VMEM_BYTES
        ),
    )(conv_input, gate, og, cw, cb[None], pw, sw, sb[None], dl, sk[None])
    outs = pl.pallas_call(
        hand_on, out_shape=kinds, in_specs=hbm, out_specs=hbm,
        scratch_shapes=[vm(k.shape, k.dtype) for k in kinds] + [dma((10,)), dma((10,))],
    )(*outs)
    flat = lambda a: a.reshape(-1)
    return (*outs[:6], flat(outs[6]), flat(outs[7]), outs[8], flat(outs[9]))


def solution(mesh):
    Z, Y = mesh.shape["ctx"], mesh.shape["chan"]

    def run(conv_input, *rest):
        cw, pw, sw, dl = rest[2], rest[4], rest[5], rest[7]
        sizes = (
            Z, Y, conv_input.shape[0] // Z, conv_input.shape[1] // Y,
            sw.shape[0], dl.shape[0], cw.shape[0],
        )
        return jax.shard_map(
            functools.partial(body, sizes), mesh=mesh, in_specs=in_specs, out_specs=out_specs,
            check_vma=False,
        )(conv_input, *rest)

    both, wide, flat = P("ctx", "chan"), P(None, "chan"), P("chan")
    in_specs = (both, both, both, wide, flat, wide, wide, flat, wide, flat)
    out_specs = (both, both, both, both, both, wide, flat, flat, wide, flat)
    return run
```
